256 devices in a mesh: tile: 32 (over x, z), pair: 8 (over y, core).
Axes of the slice: x: 4, y: 4, z: 8, core: 2. Of those that a mesh axis runs over, the one named last changes fastest.
Arguments:
- amplitudes: bfloat16 [128, 96, 512], P('pair', 'tile'), may hold values from -6 to 6
- tasks: int32 [6144, 2], P(('tile', 'pair')), may hold values from 0 to 95, as said below
- integrals: bfloat16 [6144, 512, 512], P(('tile', 'pair')), may hold values from -0.0625 to 0.0625
Outputs:
- residual: float32 [128, 96, 512], P('pair', 'tile')
The draws below stay inside these ranges and needn't reach their ends.
Inputs may be any that keep to these rules, and one draw needn't show every extreme that they name: Each row (a, c) of tasks names two tiles with a % 24 == c % 24 (so of one irrep, a % 8 == c % 8) held by different indices of tile, a // 3 != c // 3. Among the distinct tiles named by the rows of one device (aligned blocks of 24 rows, devices in the order tile, pair), at most one lies in any aligned block of 3 consecutive tiles (the tiles of one owner along tile); every device names exactly one of tiles 0, 1, 2.
All inputs are finite; a program needn't handle non-finite values.
Results may differ from the reference program's by a relative error of at most 0.0003.
Values may be sent and summed in bfloat16 or wider, within the bound.
No kernel may reach another device: no remote copies, remote signals or barrier semaphores. Data moves between devices by JAX's collectives and lax.ppermute only.
A program may use at most 128 MiB of HBM per device.

```python
import jax
import jax.numpy as jnp
from jax import lax

P_SIZE = 128
TS = 512
NK = 96
TASK_DEV = 24
TASKS = 6144
N_TILE = 32
N_PAIR = 8


def draw_tasks(key, part):
    key = jax.random.fold_in(key, 11)
    k_dev = NK // N_TILE
    slot_cap = k_dev // 3
    windows = 24 // k_dev
    residue_count = windows * slot_cap
    device_total = N_TILE * N_PAIR

    def one_device(device_index):
        device_key = jax.random.fold_in(key, device_index + 7)
        window_keys = jax.random.split(jax.random.fold_in(device_key, 2), windows)
        window_picks = jax.vmap(lambda wkey: jax.random.permutation(wkey, k_dev)[:slot_cap])(window_keys)
        residues = (window_picks + k_dev * jnp.arange(windows, dtype=jnp.int32)[:, None]).reshape(-1)
        row_ids = jnp.arange(TASK_DEV, dtype=jnp.int32)
        chosen = residues[row_ids % residue_count]
        first_m = jax.random.randint(jax.random.fold_in(device_key, 3), (TASK_DEV,), 0, 4)
        first_m = jnp.where(row_ids < slot_cap, 0, first_m)
        offset = jax.random.randint(jax.random.fold_in(device_key, 4), (TASK_DEV,), 1, 4)
        second_m = (first_m + offset) % 4
        return jnp.stack([chosen + 24 * first_m, chosen + 24 * second_m], axis=1)
    result = jax.vmap(one_device)(jnp.arange(device_total, dtype=jnp.int32))
    return result.reshape(device_total * TASK_DEV, 2).astype(jnp.int32)


def level_of(stream_key, dims, pieces, smallest, largest):
    level, own = 1.0, jax.random.fold_in(stream_key, 6)
    for axis_at, parts in pieces:
        draws = jnp.exp(jax.random.uniform(jax.random.fold_in(own, axis_at), (parts,), jnp.float32, smallest / len(pieces), largest / len(pieces)))
        level = level * jnp.repeat(draws, dims[axis_at] // parts).reshape([-1 if axis == axis_at else 1 for axis in range(len(dims))])
    return level


def gaussian(stream_key, dims, deviation, reach, cuts=(), kind=jnp.bfloat16):
    gain = level_of(stream_key, dims, cuts, -0.22, 0.18) if cuts else 1.0
    drawn = jax.random.normal(stream_key, dims, jnp.float32) * deviation * gain
    return jnp.minimum(jnp.maximum(drawn, -reach), reach).astype(kind)


def setup_inputs(seed: int = 0) -> dict:
    keys = jax.random.split(jax.random.key(seed), 4)
    return {
        "amplitudes": gaussian(keys[0], (P_SIZE, NK, TS), 1.0, 6.0, ((0, 8), (1, 32))),
        "tasks": draw_tasks(jax.random.fold_in(keys[3], 71), 0),
        "integrals": gaussian(keys[2], (TASKS, TS, TS), (16 * TS) ** -0.5, 0.0625, ((0, 256),)),
    }


def reference(amplitudes, tasks, integrals):
    def advance(total, item):
        pair_tiles, block = item
        first_tile = pair_tiles[0]
        second_tile = pair_tiles[1]
        amp_first = lax.dynamic_index_in_dim(amplitudes, first_tile, 1, keepdims=False)
        amp_second = lax.dynamic_index_in_dim(amplitudes, second_tile, 1, keepdims=False)
        term_ab = jnp.dot(amp_second, block.T, preferred_element_type=jnp.float32)
        term_cd = jnp.dot(amp_first, block, preferred_element_type=jnp.float32)
        total = total.at[:, first_tile, :].add(term_ab)
        total = total.at[:, second_tile, :].add(term_cd)
        return total, None

    start = jnp.zeros((P_SIZE, NK, TS), jnp.float32)
    residual, _ = lax.scan(advance, start, (tasks, integrals))
    return residual
```

```python
import functools

import jax
import jax.numpy as jnp
from jax import lax
from jax.experimental import pallas as pl
from jax.experimental.pallas import tpu as pltpu
from jax.sharding import PartitionSpec as P

XS, ZS, YS, CORES = 4, 8, 4, 2

LANES = 128
FULL = 32767.0
STEPS = 256.0
FLOOR = 2.0**-126
MIB = 1024 * 1024
VMEM = pl.BlockSpec(memory_space=pltpu.VMEM)
SMEM = pl.BlockSpec(memory_space=pltpu.SMEM)


def shift_x(value, by):
    table = [(t, (t // ZS + by) % XS * ZS + t % ZS) for t in range(XS * ZS)]
    return lax.ppermute(value, "tile", table)


def shift_z(value, by):
    table = [(t, t // ZS * ZS + (t + by) % ZS) for t in range(XS * ZS)]
    return lax.ppermute(value, "tile", table)


def shift_y(value, by):
    table = [(p, (p // CORES + by) % YS * CORES + p % CORES) for p in range(YS * CORES)]
    return lax.ppermute(value, "pair", table)


def other_core(value):
    return lax.ppermute(value, "pair", [(p, p ^ 1) for p in range(YS * CORES)])


def quantize(values):
    largest = jnp.max(jnp.abs(values), axis=-1, keepdims=True)
    exponent = jnp.ceil(jnp.log2(jnp.maximum(largest, FLOOR)) * STEPS)
    scaled = values * jnp.exp2(exponent * (-1.0 / STEPS)) * FULL
    codes = jnp.round(jnp.clip(scaled, -FULL, FULL)).astype(jnp.int32)
    return codes.astype(jnp.int16), exponent


def exponent_codes(exponents):
    return exponents.astype(jnp.int32).astype(jnp.int16)


def scales_of(codes):
    exponent = codes.astype(jnp.int32).astype(jnp.float32)
    return jnp.exp2(exponent * (1.0 / STEPS)) * (1.0 / FULL)


def numbers(codes):
    return codes.astype(jnp.int32).astype(jnp.float32)


def call(kernel, out_shape, in_specs):
    return pl.pallas_call(
        kernel,
        out_shape=out_shape,
        in_specs=in_specs,
        out_specs=jax.tree.map(lambda _: VMEM, out_shape),
        compiler_params=pltpu.CompilerParams(vmem_limit_bytes=24 * MIB),
    )


def pack_y_kernel(want_ref, *refs):
    own, mate, outs = refs[:XS], refs[XS : 2 * XS], refs[2 * XS :]
    rows = own[0].shape[2]
    for dy in range(YS):
        for dx in range(XS):
            for dz in range(ZS):
                slot = dx * ZS + dz
                which = want_ref[dy * XS * ZS + slot]
                outs[dy][slot, :rows] = own[dx][dz, which]
                outs[dy][slot, rows:] = mate[dx][dz, which]


def pack_x_kernel(want_ref, *refs):
    own, mate, outs = refs[:YS], refs[YS : 2 * YS], refs[2 * YS :]
    rows = own[0].shape[2]
    for dx in range(XS):
        for dz in range(ZS):
            which = want_ref[dx * XS * ZS + dx * ZS + dz]
            for dy in range(YS):
                at = dy * CORES * rows
                outs[dx][dz, at : at + rows] = own[dy][dz, which]
                outs[dx][dz, at + rows : at + 2 * rows] = mate[dy][dz, which]


def pack_y(want, own, mate):
    _, _, rows, width = own[0].shape
    out = [jax.ShapeDtypeStruct((XS * ZS, CORES * rows, width), own[0].dtype)] * YS
    return call(pack_y_kernel, out, [SMEM] + [VMEM] * (2 * XS))(want, *own, *mate)


def pack_x(want, own, mate):
    _, _, rows, width = own[0].shape
    out = [jax.ShapeDtypeStruct((ZS, YS * CORES * rows, width), own[0].dtype)] * XS
    return call(pack_x_kernel, out, [SMEM] + [VMEM] * (2 * YS))(want, *own, *mate)


def contract_kernel(slot_ref, *refs):
    from_y, refs = refs[:YS], refs[YS:]
    from_x, refs = refs[:XS], refs[XS:]
    block_ref, refs = refs[0], refs[1:]
    to_y, refs = refs[:YS], refs[YS:]
    to_x, refs = refs[:XS], refs[XS:]
    amp, total, arrived = refs
    step = pl.program_id(0)
    slots, rows, width = amp.shape
    half = width // 2
    chunks = half // LANES
    per_y = rows // YS

    @pl.when(step == 0)
    def _():
        copies = []
        for dy in range(YS):
            target = amp.at[:, dy * per_y : (dy + 1) * per_y, :half]
            copies.append(pltpu.make_async_copy(from_y[dy], target, arrived.at[dy]))
        for dx in range(XS):
            target = amp.at[dx * ZS : (dx + 1) * ZS, :, half:]
            copies.append(pltpu.make_async_copy(from_x[dx], target, arrived.at[YS + dx]))
        for copy in copies:
            copy.start()
        total[...] = jnp.zeros_like(total)
        for copy in copies:
            copy.wait()

    for at in range(block_ref.shape[0]):
        task = step * block_ref.shape[0] + at
        first = slot_ref[2 * task]
        second = slot_ref[2 * task + 1]
        block = block_ref[at]
        total[first] += lax.dot_general(
            amp[second], block, (((1,), (1,)), ((), ())), preferred_element_type=jnp.float32
        )
        total[second] += jnp.dot(amp[first], block, preferred_element_type=jnp.float32)

    @pl.when(step == pl.num_programs(0) - 1)
    def _():
        lane = lax.broadcasted_iota(jnp.int32, (rows, LANES), 1)
        blank = jnp.zeros((rows, LANES), jnp.float32)
        exponents_y = blank
        for dx in range(XS):

            def one_slot(dz, exponents, dx=dx):
                exponents_y, exponents_x = exponents
                slot = dx * ZS + dz
                codes, exponent = quantize(total[slot, :, :half])
                for dy in range(YS):
                    for chunk in range(chunks):
                        to_y[dy][slot * chunks + chunk] = codes[
                            dy * per_y : (dy + 1) * per_y, chunk * LANES : (chunk + 1) * LANES
                        ]
                exponents_y = jnp.where(lane == slot, exponent, exponents_y)
                codes, exponent = quantize(total[slot, :, half:])
                for chunk in range(chunks):
                    to_x[dx][dz * chunks + chunk] = codes[:, chunk * LANES : (chunk + 1) * LANES]
                return exponents_y, jnp.where(lane == dz, exponent, exponents_x)

            exponents_y, exponents_x = lax.fori_loop(0, ZS, one_slot, (exponents_y, blank))
            to_x[dx][ZS * chunks] = exponent_codes(exponents_x)
        for dy in range(YS):
            to_y[dy][slots * chunks] = exponent_codes(exponents_y[dy * per_y : (dy + 1) * per_y])


def contract(slots, from_y, from_x, blocks, per_step):
    slot_count, per_y, half = from_y[0].shape
    rows = from_x[0].shape[1]
    tasks, width, _ = blocks.shape
    chunks = half // LANES
    out_y = (slot_count * chunks + 1, per_y, LANES)
    out_x = (ZS * chunks + 1, rows, LANES)
    whole = lambda t, *_: (0, 0, 0)
    found = pl.pallas_call(
        contract_kernel,
        out_shape=[jax.ShapeDtypeStruct(out_y, jnp.int16)] * YS
        + [jax.ShapeDtypeStruct(out_x, jnp.int16)] * XS,
        grid_spec=pltpu.PrefetchScalarGridSpec(
            num_scalar_prefetch=1,
            grid=(tasks // per_step,),
            in_specs=[pl.BlockSpec(memory_space=pl.ANY)] * (YS + XS)
            + [pl.BlockSpec((per_step, width, width), lambda t, *_: (t, 0, 0))],
            out_specs=[pl.BlockSpec(out_y, whole)] * YS + [pl.BlockSpec(out_x, whole)] * XS,
            scratch_shapes=[
                pltpu.VMEM((slot_count, rows, width), blocks.dtype),
                pltpu.VMEM((slot_count, rows, width), jnp.float32),
                pltpu.SemaphoreType.DMA((YS + XS,)),
            ],
        ),
        compiler_params=pltpu.CompilerParams(vmem_limit_bytes=40 * MIB),
    )(slots, *from_y, *from_x, blocks)
    return found[:YS], found[YS:]


def combine_y_kernel(want_ref, *refs):
    pieces, (mine, theirs) = refs[:YS], refs[YS:]
    slots = XS * ZS
    tiles, rows, half = mine.shape
    per_owner = tiles // slots
    chunks = half // LANES
    mine[...] = jnp.zeros_like(mine)
    theirs[...] = jnp.zeros_like(theirs)
    for dy in range(YS):
        scales = scales_of(pieces[dy][slots * chunks])
        for slot in range(slots):
            tile = slot * per_owner + want_ref[dy * slots + slot]
            for chunk in range(chunks):
                lanes = slice(chunk * LANES, (chunk + 1) * LANES)
                found = numbers(pieces[dy][slot * chunks + chunk]) * scales[:, slot : slot + 1]
                mine[tile, :, lanes] += found[:rows]
                theirs[tile, :, lanes] += found[rows:]


def combine_x_kernel(want_ref, *refs):
    pieces, (mine, theirs) = refs[:XS], refs[XS:]
    slots = XS * ZS
    tiles, _, rows, half = mine.shape
    per_owner = tiles // ZS
    chunks = half // LANES
    mine[...] = jnp.zeros_like(mine)
    theirs[...] = jnp.zeros_like(theirs)
    for dx in range(XS):
        scales = scales_of(pieces[dx][ZS * chunks])
        for dz in range(ZS):
            tile = dz * per_owner + want_ref[dx * slots + dx * ZS + dz]
            for chunk in range(chunks):
                lanes = slice(chunk * LANES, (chunk + 1) * LANES)
                found = numbers(pieces[dx][dz * chunks + chunk]) * scales[:, dz : dz + 1]
                found = found.reshape(YS, CORES, rows, LANES)
                mine[tile, :, :, lanes] += found[:, 0]
                theirs[tile, :, :, lanes] += found[:, 1]


def split_kernel(tile_of, mine, got, *outs):
    count, rows, _ = outs[0].shape
    chunks = mine.shape[-1] // LANES
    count //= chunks
    lane = lax.broadcasted_iota(jnp.int32, (rows, LANES), 1)
    for away, out in enumerate(outs):
        exponents = jnp.zeros((rows, LANES), jnp.float32)
        for tile in range(count):
            at = tile_of(away, tile)
            codes, exponent = quantize(mine[at] + got[at])
            for chunk in range(chunks):
                out[tile * chunks + chunk] = codes[:, chunk * LANES : (chunk + 1) * LANES]
            exponents = jnp.where(lane == tile, exponent, exponents)
        out[count * chunks] = exponent_codes(exponents)


def regroup_kernel(per_owner, *refs):
    halves, outs = (refs[:XS], refs[XS : XS + YS]), refs[XS + YS :]
    count, rows, _ = halves[0][0].shape
    chunks = (count - 1) // (per_owner * ZS)
    lane = lax.broadcasted_iota(jnp.int32, (rows, LANES), 1)
    scales = [[scales_of(piece[count - 1]) for piece in pieces] for pieces in halves]
    for dz in range(ZS):
        exponents = jnp.zeros((rows, LANES), jnp.float32)
        for which in range(per_owner):
            tile = dz * per_owner + which
            for part, pieces in enumerate(halves):
                found = 0.0
                for piece, scale in zip(pieces, scales[part]):
                    codes = [numbers(piece[tile * chunks + chunk]) for chunk in range(chunks)]
                    found += jnp.concatenate(codes, axis=-1) * scale[:, tile : tile + 1]
                codes, exponent = quantize(found)
                at = which * 2 + part
                for chunk in range(chunks):
                    outs[dz][at * chunks + chunk] = codes[:, chunk * LANES : (chunk + 1) * LANES]
                exponents = jnp.where(lane == at, exponent, exponents)
        outs[dz][per_owner * 2 * chunks] = exponent_codes(exponents)


def finish_kernel(*refs):
    pieces, out = refs[:-1], refs[-1]
    per_owner, _, width = out.shape
    chunks = width // LANES
    scales = [scales_of(piece[per_owner * chunks]) for piece in pieces]
    for which in range(per_owner):
        for chunk in range(chunks):
            at = which * 2 + chunk * 2 // chunks
            found = 0.0
            for piece, scale in zip(pieces, scales):
                found += numbers(piece[which * chunks + chunk]) * scale[:, at : at + 1]
            out[which, :, chunk * LANES : (chunk + 1) * LANES] = found


def local(amplitudes, tasks, integrals):
    rows, per_owner, width = amplitudes.shape
    half = width // 2
    chunks = half // LANES
    slot_count = XS * ZS
    place = lax.axis_index("tile")
    x, z = place // ZS, place % ZS

    names = tasks.reshape(-1)
    owner = names // per_owner
    slots = (x - owner // ZS) % XS * ZS + (z - owner) % ZS
    is_slot = slots[:, None] == jnp.arange(slot_count, dtype=jnp.int32)[None, :]
    want = jnp.max(jnp.where(is_slot, names[:, None] % per_owner, 0), axis=0)
    wants_y = jnp.concatenate([want] + [shift_y(want, -d) for d in range(1, YS)])
    wants_x = jnp.concatenate([want] + [shift_x(want, -d) for d in range(1, XS)])

    tiles = amplitudes.transpose(1, 0, 2)
    along_z = jnp.stack([tiles] + [shift_z(tiles, d) for d in range(1, ZS)])
    low, high = along_z[..., :half], along_z[..., half:]
    along_x = [low] + [shift_x(low, d) for d in range(1, XS)]
    along_y = [high] + [shift_y(high, d) for d in range(1, YS)]
    mate_x = [other_core(v) for v in along_x]
    mate_y = [other_core(v) for v in along_y]
    packed_y = pack_y(wants_y, along_x, mate_x)
    packed_x = pack_x(wants_x, along_y, mate_y)
    from_y = [packed_y[0]] + [shift_y(packed_y[d], d) for d in range(1, YS)]
    from_x = [packed_x[0]] + [shift_x(packed_x[d], d) for d in range(1, XS)]

    to_y, to_x = contract(slots, from_y, from_x, integrals, 4)

    back_y = [to_y[0]] + [shift_y(to_y[d], -d) for d in range(1, YS)]
    back_x = [to_x[0]] + [shift_x(to_x[d], -d) for d in range(1, XS)]
    sums = jax.ShapeDtypeStruct((slot_count * per_owner, rows, half), jnp.float32)
    mine_y, theirs_y = call(combine_y_kernel, [sums] * 2, [SMEM] + [VMEM] * YS)(wants_y, *back_y)
    sums = jax.ShapeDtypeStruct((ZS * per_owner, YS, rows, half), jnp.float32)
    mine_x, theirs_x = call(combine_x_kernel, [sums] * 2, [SMEM] + [VMEM] * XS)(wants_x, *back_x)
    got_y, got_x = other_core(theirs_y), other_core(theirs_x)

    count = ZS * per_owner
    cut = jax.ShapeDtypeStruct((count * chunks + 1, rows, LANES), jnp.int16)
    split_x = call(
        functools.partial(split_kernel, lambda away, tile: away * count + tile), [cut] * XS, [VMEM] * 2
    )(mine_y, got_y)
    split_y = call(
        functools.partial(split_kernel, lambda away, tile: (tile, away)), [cut] * YS, [VMEM] * 2
    )(mine_x, got_x)
    split_x = [split_x[0]] + [shift_x(split_x[d], -d) for d in range(1, XS)]
    split_y = [split_y[0]] + [shift_y(split_y[d], -d) for d in range(1, YS)]

    cut = jax.ShapeDtypeStruct((per_owner * 2 * chunks + 1, rows, LANES), jnp.int16)
    split_z = call(functools.partial(regroup_kernel, per_owner), [cut] * ZS, [VMEM] * (XS + YS))(*split_x, *split_y)
    split_z = [split_z[0]] + [shift_z(split_z[d], -d) for d in range(1, ZS)]
    out = jax.ShapeDtypeStruct((per_owner, rows, width), jnp.float32)
    return call(finish_kernel, out, [VMEM] * ZS)(*split_z).transpose(1, 0, 2)


def solution(mesh):
    return jax.shard_map(
        local,
        mesh=mesh,
        in_specs=(
            P("pair", "tile", None),
            P(("tile", "pair"), None),
            P(("tile", "pair"), None, None),
        ),
        out_specs=P("pair", "tile", None),
        check_vma=False,
    )
```

```python
import jax
import jax.numpy as jnp
from jax import lax
from jax.experimental import pallas as pl
from jax.experimental.pallas import tpu as pltpu
from jax.sharding import Mesh
from jax.sharding import PartitionSpec as P

XS, ZS, YS, CORES = 4, 8, 4, 2
PLANE = ("x", "y", "core")
PER_STEP = 8

LANES = 128
FULL = 32767.0
STEPS = 256.0
FLOOR = 2.0**-110
MIB = 1024 * 1024
VMEM = pl.BlockSpec(memory_space=pltpu.VMEM)
SMEM = pl.BlockSpec(memory_space=pltpu.SMEM)


def shift_z(value, by):
    return lax.ppermute(value, "z", [(z, (z + by) % ZS) for z in range(ZS)])


def swap(value, axes):
    return lax.all_to_all(value, axes, split_axis=0, concat_axis=0, tiled=True)


def quantize(values):
    largest = jnp.max(jnp.abs(values), axis=-1, keepdims=True)
    exponent = jnp.ceil(jnp.log2(jnp.maximum(largest, FLOOR)) * STEPS)
    codes = jnp.round(values * (jnp.exp2(exponent * (-1.0 / STEPS)) * FULL)).astype(jnp.int32)
    return codes.astype(jnp.int16), exponent


def exponent_codes(exponents):
    return exponents.astype(jnp.int32).astype(jnp.int16)


def numbers(codes):
    return codes.astype(jnp.int32).astype(jnp.float32)


def scales_of(codes):
    return jnp.exp2(numbers(codes) * (1.0 / STEPS)) * (1.0 / FULL)


def call(kernel, out_shape, in_specs):
    return pl.pallas_call(
        kernel,
        out_shape=out_shape,
        in_specs=in_specs,
        out_specs=jax.tree.map(lambda _: VMEM, out_shape),
        compiler_params=pltpu.CompilerParams(vmem_limit_bytes=24 * MIB),
    )


def pack_kernel(want_ref, *refs):
    along_z, out = refs[:-1], refs[-1]

    def one(dest, carry):
        for dz, tiles in enumerate(along_z):
            out[dest, dz] = tiles[want_ref[dest * ZS + dz]]
        return carry

    lax.fori_loop(0, out.shape[0], one, 0)


def contract_kernel(slot_ref, amp_ref, block_ref, out_ref, total):
    step = pl.program_id(0)
    slots, rows, width = total.shape
    peers, part = rows // amp_ref.shape[2], amp_ref.shape[2]
    chunks = width // LANES

    @pl.when(step == 0)
    def _():
        total[...] = jnp.zeros_like(total)

    def amplitudes(slot):
        return amp_ref[pl.ds(slot // ZS * peers, peers), slot % ZS].reshape(rows, width)

    for at in range(block_ref.shape[0]):
        task = step * block_ref.shape[0] + at
        first = slot_ref[2 * task]
        second = slot_ref[2 * task + 1]
        block = block_ref[at]
        total[first] += lax.dot_general(
            amplitudes(second), block, (((1,), (1,)), ((), ())), preferred_element_type=jnp.float32
        )
        total[second] += jnp.dot(amplitudes(first), block, preferred_element_type=jnp.float32)

    @pl.when(step == pl.num_programs(0) - 1)
    def _():
        lane = lax.broadcasted_iota(jnp.int32, (rows, LANES), 1)

        def one_x(x, carry):
            exponents = jnp.zeros((rows, LANES), jnp.float32)
            to = pl.ds(x * peers, peers)
            for dz in range(ZS):
                codes, exponent = quantize(total[x * ZS + dz])
                codes = codes.reshape(peers, part, width)
                for chunk in range(chunks):
                    out_ref[to, dz * chunks + chunk] = codes[..., chunk * LANES : (chunk + 1) * LANES]
                exponents = jnp.where(lane == dz, exponent, exponents)
            out_ref[to, ZS * chunks] = exponent_codes(exponents).reshape(peers, part, LANES)
            return carry

        lax.fori_loop(0, slots // ZS, one_x, 0)


def contract(slots, amp, blocks):
    devices, _, part, width = amp.shape
    tasks = blocks.shape[0]
    out = (devices, ZS * (width // LANES) + 1, part, LANES)
    return pl.pallas_call(
        contract_kernel,
        out_shape=jax.ShapeDtypeStruct(out, jnp.int16),
        grid_spec=pltpu.PrefetchScalarGridSpec(
            num_scalar_prefetch=1,
            grid=(tasks // PER_STEP,),
            in_specs=[
                pl.BlockSpec(amp.shape, lambda t, *_: (0, 0, 0, 0)),
                pl.BlockSpec((PER_STEP, width, width), lambda t, *_: (t, 0, 0)),
            ],
            out_specs=pl.BlockSpec(out, lambda t, *_: (0, 0, 0, 0)),
            scratch_shapes=[
                pltpu.VMEM((XS * ZS, devices // XS * part, width), jnp.float32),
            ],
        ),
        compiler_params=pltpu.CompilerParams(vmem_limit_bytes=40 * MIB),
    )(slots, amp, blocks)


def combine_kernel(want_ref, place_ref, pieces, out, total):
    devices, count, rows, _ = pieces.shape
    tiles, _, width = total.shape
    per_owner = tiles // ZS
    chunks = width // LANES
    lane = lax.broadcasted_iota(jnp.int32, (rows, LANES), 1)
    total[...] = jnp.zeros_like(total)

    def one_device(device, carry):
        scales = scales_of(pieces[device, count - 1])
        for dz in range(ZS):
            tile = dz * per_owner + want_ref[device * ZS + dz]
            scale = scales[:, dz : dz + 1]
            for chunk in range(chunks):
                lanes = slice(chunk * LANES, (chunk + 1) * LANES)
                total[tile, :, lanes] += numbers(pieces[device, dz * chunks + chunk]) * scale
        return carry

    lax.fori_loop(0, devices, one_device, 0)

    for dz in range(ZS):
        to = lax.rem(place_ref[0] + (ZS - dz), ZS)
        exponents = jnp.zeros((rows, LANES), jnp.float32)
        for which in range(per_owner):
            codes, exponent = quantize(total[dz * per_owner + which])
            for chunk in range(chunks):
                out[to, which * chunks + chunk] = codes[:, chunk * LANES : (chunk + 1) * LANES]
            exponents = jnp.where(lane == which, exponent, exponents)
        out[to, per_owner * chunks] = exponent_codes(exponents)


def combine(want, place, pieces, per_owner, width):
    _, _, rows, _ = pieces.shape
    out = (ZS, per_owner * (width // LANES) + 1, rows, LANES)
    return pl.pallas_call(
        combine_kernel,
        out_shape=jax.ShapeDtypeStruct(out, jnp.int16),
        in_specs=[SMEM, SMEM, VMEM],
        out_specs=VMEM,
        scratch_shapes=[pltpu.VMEM((ZS * per_owner, rows, width), jnp.float32)],
        compiler_params=pltpu.CompilerParams(vmem_limit_bytes=24 * MIB),
    )(want, place, pieces)


def finish_kernel(pieces, out):
    per_owner, _, width = out.shape
    chunks = width // LANES
    scales = [scales_of(pieces[z, per_owner * chunks]) for z in range(ZS)]
    for which in range(per_owner):
        for chunk in range(chunks):
            found = 0.0
            for z, scale in enumerate(scales):
                found += numbers(pieces[z, which * chunks + chunk]) * scale[:, which : which + 1]
            out[which, :, chunk * LANES : (chunk + 1) * LANES] = found


def local(amplitudes, tasks, integrals):
    rows, per_owner, width = amplitudes.shape
    peers = YS * CORES
    z = lax.axis_index("z")

    names = tasks.reshape(-1)
    owner = names // per_owner
    slots = owner // ZS * ZS + (z - owner) % ZS
    is_slot = slots[:, None] == jnp.arange(XS * ZS, dtype=jnp.int32)[None, :]
    want = jnp.max(jnp.where(is_slot, names[:, None] % per_owner, 0), axis=0)

    tiles = amplitudes.transpose(1, 0, 2)
    along_z = [tiles] + [shift_z(tiles, d) for d in range(1, ZS)]
    want = jnp.broadcast_to(want.reshape(XS, 1, ZS), (XS, peers, ZS)).reshape(XS * peers, ZS)
    wants = swap(want, PLANE).reshape(-1)
    packed = jax.ShapeDtypeStruct((XS * peers, ZS, rows, width), tiles.dtype)
    packed = call(pack_kernel, packed, [SMEM] + [VMEM] * ZS)(wants, *along_z)
    partial_sums = contract(slots, swap(packed, PLANE), integrals)
    by_place = combine(wants, z.reshape(1), swap(partial_sums, PLANE), per_owner, width)
    returned = swap(by_place, "z")
    out = jax.ShapeDtypeStruct((per_owner, rows, width), jnp.float32)
    return call(finish_kernel, out, [VMEM])(returned).transpose(1, 0, 2)


def solution(mesh):
    fine = Mesh(mesh.devices.reshape(XS, ZS, YS, CORES), ("x", "z", "y", "core"))
    tile, pair = ("x", "z"), ("y", "core")
    return jax.shard_map(
        local,
        mesh=fine,
        in_specs=(P(pair, tile, None), P(tile + pair, None), P(tile + pair, None, None)),
        out_specs=P(pair, tile, None),
        check_vma=False,
    )
```

```python
import jax
import jax.numpy as jnp
from jax import lax
from jax.experimental import pallas as pl
from jax.experimental.pallas import tpu as pltpu
from jax.sharding import Mesh
from jax.sharding import PartitionSpec as P

XS, ZS, YS, CORES = 4, 8, 4, 2
PLANE = ("x", "y", "core")
WHOLE = ("x", "z", "y", "core")
PER_STEP = 8
CHUNKS = 2

LANES = 128
FULL = 32767.0
STEPS = 256.0
FLOOR = 2.0**-110
MIB = 1024 * 1024
VMEM = pl.BlockSpec(memory_space=pltpu.VMEM)
SMEM = pl.BlockSpec(memory_space=pltpu.SMEM)


def swap(value, axes):
    return lax.all_to_all(value, axes, split_axis=0, concat_axis=0, tiled=True)


def quantize(values):
    largest = jnp.max(jnp.abs(values), axis=-1, keepdims=True)
    exponent = jnp.ceil(jnp.log2(jnp.maximum(largest, FLOOR)) * STEPS)
    codes = jnp.round(values * (jnp.exp2(exponent * (-1.0 / STEPS)) * FULL)).astype(jnp.int32)
    return codes.astype(jnp.int16), exponent


def exponent_codes(exponents):
    return exponents.astype(jnp.int32).astype(jnp.int16)


def numbers(codes):
    return codes.astype(jnp.int32).astype(jnp.float32)


def scales_of(codes):
    return jnp.exp2(numbers(codes) * (1.0 / STEPS)) * (1.0 / FULL)


def call(kernel, out_shape, in_specs, scratch=()):
    return pl.pallas_call(
        kernel,
        out_shape=out_shape,
        in_specs=in_specs,
        out_specs=jax.tree.map(lambda _: VMEM, out_shape),
        scratch_shapes=scratch,
        compiler_params=pltpu.CompilerParams(vmem_limit_bytes=24 * MIB),
    )


def device(x, z, y, core):
    return ((x % XS * ZS + z) * YS + y % YS) * CORES + core


def move(value, by, near):
    table = []
    for x in range(XS):
        for z in range(ZS):
            for y in range(YS):
                for core in range(CORES):
                    along_x = (core == 0) == near
                    to = device(x + by * along_x, z, y + by * (not along_x), core)
                    table.append((device(x, z, y, core), to))
    return lax.ppermute(value, WHOLE, table)


def trade(value):
    return lax.ppermute(value, "core", [(0, 1), (1, 0)])


def far_device(place_ref, far, side):
    x, y, core = place_ref[0], place_ref[1], place_ref[2]
    x = (x + far * core) & (XS - 1)
    y = (y + far * (1 - core)) & (YS - 1)
    return (x * YS + y) * CORES + (core ^ side)


def pack_kernel(place_ref, want_ref, *refs):
    gathered, outs = refs[:XS], refs[XS:]
    core = place_ref[2]
    for side in range(CORES):
        for far in range(XS):
            row = far_device(place_ref, far, side)
            for near in range(XS):
                slot = (near + core * (far - near)) * ZS
                for z in range(ZS):
                    outs[side * XS + far][near * ZS + z] = gathered[near][z, want_ref[row, slot + z]]


def contract_kernel(slot_ref, place_ref, *refs):
    pieces, block_ref, outs = refs[: 2 * XS], refs[2 * XS], refs[2 * XS + 1 : 4 * XS + 1]
    amp, total, arrived = refs[4 * XS + 1 :]
    step = pl.program_id(0)
    _, slots, rows, half = total.shape
    part = rows // YS
    chunks = half // LANES

    def spot(side, far, near):
        core = place_ref[2] ^ side
        slot = pl.multiple_of((near + core * (far - near)) * ZS, ZS)
        return core, slot, pl.multiple_of((far + core * (near - far)) * part, part)

    @pl.when(step == 0)
    def _():
        copies = []
        for side in range(CORES):
            for far in range(XS):
                for near in range(XS):
                    at, slot, row = spot(side, far, near)
                    copies.append(
                        pltpu.make_async_copy(
                            pieces[side * XS + far].at[pl.ds(near * ZS, ZS)],
                            amp.at[at, pl.ds(slot, ZS), pl.ds(row, part)],
                            arrived.at[len(copies)],
                        )
                    )
        for copy in copies:
            copy.start()
        total[...] = jnp.zeros_like(total)
        for copy in copies:
            copy.wait()

    def amplitudes(slot):
        return jnp.concatenate([amp[0, slot], amp[1, slot]], axis=1)

    for at in range(block_ref.shape[0]):
        task = step * block_ref.shape[0] + at
        first = slot_ref[2 * task]
        second = slot_ref[2 * task + 1]
        block = block_ref[at]
        term = lax.dot_general(
            amplitudes(second), block, (((1,), (1,)), ((), ())), preferred_element_type=jnp.float32
        )
        total[0, first] += term[:, :half]
        total[1, first] += term[:, half:]
        term = jnp.dot(amplitudes(first), block, preferred_element_type=jnp.float32)
        total[0, second] += term[:, :half]
        total[1, second] += term[:, half:]

    @pl.when(step == pl.num_programs(0) - 1)
    def _():
        lane = lax.broadcasted_iota(jnp.int32, (part, LANES), 1)
        for side in range(CORES):
            for far in range(XS):
                out = outs[side * XS + far]

                def some_entries(near, exponents):
                    at, slot, row = spot(side, far, near)
                    for z in range(ZS):
                        entry = near * ZS + z
                        codes, exponent = quantize(total[at, slot + z, pl.ds(row, part)])
                        for chunk in range(chunks):
                            out[entry * chunks + chunk] = codes[:, chunk * LANES : (chunk + 1) * LANES]
                        exponents = jnp.where(lane == entry, exponent, exponents)
                    return exponents

                exponents = lax.fori_loop(0, XS, some_entries, jnp.zeros((part, LANES), jnp.float32))
                out[slots * chunks] = exponent_codes(exponents)


def contract(slots, place, pieces, blocks):
    entries, part, half = pieces[0].shape
    tasks, width, _ = blocks.shape
    out = (entries * (half // LANES) + 1, part, LANES)
    halves = (CORES, entries, YS * part, half)
    return pl.pallas_call(
        contract_kernel,
        out_shape=[jax.ShapeDtypeStruct(out, jnp.int16)] * (2 * XS),
        grid_spec=pltpu.PrefetchScalarGridSpec(
            num_scalar_prefetch=2,
            grid=(tasks // PER_STEP,),
            in_specs=[pl.BlockSpec(memory_space=pl.ANY)] * (2 * XS)
            + [pl.BlockSpec((PER_STEP, width, width), lambda t, *_: (t, 0, 0))],
            out_specs=[pl.BlockSpec(out, lambda t, *_: (0, 0, 0))] * (2 * XS),
            scratch_shapes=[
                pltpu.VMEM(halves, blocks.dtype),
                pltpu.VMEM(halves, jnp.float32),
                pltpu.SemaphoreType.DMA((CORES * XS * XS,)),
            ],
        ),
        compiler_params=pltpu.CompilerParams(vmem_limit_bytes=40 * MIB),
    )(slots, place, *pieces, blocks)


def encode(rows_of, count, out, rows, place=()):
    lane = lax.broadcasted_iota(jnp.int32, (rows, LANES), 1)
    exponents = jnp.zeros((rows, LANES), jnp.float32)
    for tile in range(count):
        codes, exponent = quantize(rows_of(tile))
        chunks = codes.shape[-1] // LANES
        for chunk in range(chunks):
            out[*place, tile * chunks + chunk] = codes[:, chunk * LANES : (chunk + 1) * LANES]
        exponents = jnp.where(lane == tile, exponent, exponents)
    out[*place, count * chunks] = exponent_codes(exponents)


def combine_kernel(place_ref, want_ref, *refs):
    pieces, outs, totals = refs[: 2 * XS], refs[2 * XS : 3 * XS], refs[3 * XS :]
    core = place_ref[2]
    tiles, rows, half = totals[0].shape
    per_owner = tiles // ZS
    chunks = half // LANES
    for total in totals:
        total[...] = jnp.zeros_like(total)
    for side in range(CORES):
        for far in range(XS):
            piece = pieces[side * XS + far]
            row = far_device(place_ref, far, side)
            scales = scales_of(piece[XS * ZS * chunks])
            for z in range(ZS):
                for near, total in enumerate(totals):
                    entry = near * ZS + z
                    slot = (near + core * (far - near)) * ZS
                    tile = z * per_owner + want_ref[row, slot + z]
                    scale = jnp.broadcast_to(scales[:, entry : entry + 1], (rows, LANES))
                    for chunk in range(chunks):
                        lanes = slice(chunk * LANES, (chunk + 1) * LANES)
                        total[tile, :, lanes] += numbers(piece[entry * chunks + chunk]) * scale
    for total, out in zip(totals, outs):
        encode(lambda tile: total[tile], tiles, out, rows)


def regroup_kernel(*refs):
    pieces, out = refs[:XS], refs[XS]
    count, rows, _ = pieces[0].shape
    per_owner = (out.shape[1] - 1) // CHUNKS
    scales = [scales_of(piece[count - 1]) for piece in pieces]
    for z in range(ZS):

        def rows_of(which):
            tile = z * per_owner + which
            found = [0.0] * CHUNKS
            for piece, scale in zip(pieces, scales):
                scale = jnp.broadcast_to(scale[:, tile : tile + 1], (rows, LANES))
                for chunk in range(CHUNKS):
                    found[chunk] += numbers(piece[tile * CHUNKS + chunk]) * scale
            return jnp.concatenate(found, axis=1)

        encode(rows_of, per_owner, out, rows, (z,))


def finish_kernel(place_ref, pieces, keep, send):
    per_owner, rows, _ = keep.shape
    mine = pl.multiple_of(place_ref[2] * rows, rows)
    for out, row in ((keep, mine), (send, rows - mine)):
        row = pl.multiple_of(row, rows)
        scales = [scales_of(pieces[z, per_owner * CHUNKS, pl.ds(row, rows)]) for z in range(ZS)]
        for which in range(per_owner):
            for chunk in range(CHUNKS):
                found = 0.0
                for z, scale in enumerate(scales):
                    codes = numbers(pieces[z, which * CHUNKS + chunk, pl.ds(row, rows)])
                    found += codes * scale[:, which : which + 1]
                out[which, :, chunk * LANES : (chunk + 1) * LANES] = found


def local(amplitudes, tasks, integrals):
    rows, per_owner, width = amplitudes.shape
    half = width // 2
    entries = XS * ZS
    part = CORES * rows
    kind = amplitudes.dtype
    place = jnp.stack([lax.axis_index(axis) for axis in PLANE]).astype(jnp.int32)
    x, core = place[0], place[2]

    def in_order(own, other, axis):
        found = jnp.concatenate([own, other], axis=axis)
        return jnp.where(core == 0, found, jnp.concatenate([other, own], axis=axis))

    tiles = amplitudes.transpose(1, 0, 2)
    low, high = tiles[..., :half], tiles[..., half:]
    own, other = jnp.where(core == 0, low, high), jnp.where(core == 0, high, low)
    tiles = in_order(own, trade(other), 1)
    along_z = swap(jnp.broadcast_to(tiles[None], (ZS, *tiles.shape)), "z")
    gathered = [along_z] + [move(along_z, near, True) for near in range(1, XS)]

    names = tasks.reshape(-1)
    owner = names * 171 >> 9
    slots = ((x - (owner // ZS)) & (XS - 1)) * ZS + (owner & (ZS - 1))
    lane = lax.broadcasted_iota(jnp.int32, (names.shape[0], LANES), 1)
    which = (names - owner * per_owner)[:, None]
    want = jnp.max(jnp.where(slots[:, None] == lane, which, 0), axis=0)
    devices = XS * YS * CORES
    wants = swap(jnp.broadcast_to(want, (devices, 1, LANES)), PLANE).reshape(devices, LANES)

    piece = jax.ShapeDtypeStruct((entries, part, half), kind)
    packed = call(pack_kernel, [piece] * (2 * XS), [SMEM] * 2 + [VMEM] * XS)(place, wants, *gathered)
    direct, via = packed[:XS], packed[XS:]
    via = [trade(v if far == 0 else move(v, far, False)) for far, v in enumerate(via)]
    direct = [v if far == 0 else move(v, far, False) for far, v in enumerate(direct)]

    codes = contract(slots, place, direct + via, integrals)

    via = [trade(v) for v in codes[XS:]]
    via = [v if far == 0 else move(v, -far, False) for far, v in enumerate(via)]
    direct = [v if far == 0 else move(v, -far, False) for far, v in enumerate(codes[:XS])]
    tile_count = ZS * per_owner
    cut = jax.ShapeDtypeStruct((tile_count * CHUNKS + 1, part, LANES), jnp.int16)
    by_near = call(
        combine_kernel,
        [cut] * XS,
        [SMEM] * 2 + [VMEM] * (2 * XS),
        [pltpu.VMEM((tile_count, part, half), jnp.float32)] * XS,
    )(place, wants, *direct, *via)
    by_near = [v if near == 0 else move(v, -near, True) for near, v in enumerate(by_near)]
    cut = jax.ShapeDtypeStruct((ZS, per_owner * CHUNKS + 1, part, LANES), jnp.int16)
    by_z = swap(call(regroup_kernel, cut, [VMEM] * XS)(*by_near), "z")
    out = jax.ShapeDtypeStruct((per_owner, rows, half), jnp.float32)
    keep, send = call(finish_kernel, [out] * 2, [SMEM, VMEM])(place, by_z)
    return in_order(keep, trade(send), 2).transpose(1, 0, 2)


def solution(mesh):
    fine = Mesh(mesh.devices.reshape(XS, ZS, YS, CORES), ("x", "z", "y", "core"))
    tile, pair = ("x", "z"), ("y", "core")
    return jax.shard_map(
        local,
        mesh=fine,
        in_specs=(P(pair, tile, None), P(tile + pair, None), P(tile + pair, None, None)),
        out_specs=P(pair, tile, None),
        check_vma=False,
    )
```

```python
import jax
import jax.numpy as jnp
from jax import lax
from jax.experimental import pallas as pl
from jax.experimental.pallas import tpu as pltpu
from jax.sharding import Mesh
from jax.sharding import PartitionSpec as P

XS, ZS, YS, CORES = 4, 8, 4, 2
PLANE = ("x", "y", "core")
WHOLE = ("x", "z", "y", "core")
PER_STEP = 8

LANES = 128
FULL = 32767.0
STEPS = 256.0
FLOOR = 2.0**-110
MIB = 1024 * 1024
VMEM = pl.BlockSpec(memory_space=pltpu.VMEM)
SMEM = pl.BlockSpec(memory_space=pltpu.SMEM)


def swap(value, axes):
    return lax.all_to_all(value, axes, split_axis=0, concat_axis=0, tiled=True)


def exponents_of(largest):
    return jnp.ceil(jnp.log2(jnp.maximum(largest, FLOOR)) * STEPS)


def exponent_codes(exponents):
    return exponents.astype(jnp.int32).astype(jnp.int16)


def numbers(codes):
    return codes.astype(jnp.int32).astype(jnp.float32)


def scales_of(codes):
    return jnp.exp2(numbers(codes) * (1.0 / STEPS)) * (1.0 / FULL)


def call(kernel, out_shape, in_specs, scratch=()):
    return pl.pallas_call(
        kernel,
        out_shape=out_shape,
        in_specs=in_specs,
        out_specs=jax.tree.map(lambda _: VMEM, out_shape),
        scratch_shapes=scratch,
        compiler_params=pltpu.CompilerParams(vmem_limit_bytes=24 * MIB),
    )


def device(x, z, y, core):
    return ((x % XS * ZS + z) * YS + y % YS) * CORES + core


def move(value, by, near, cross=0):
    table = []
    for x in range(XS):
        for z in range(ZS):
            for y in range(YS):
                for core in range(CORES):
                    along_x = (core == 0) == near
                    to = device(x + by * along_x, z, y + by * (not along_x), core ^ cross)
                    table.append((device(x, z, y, core), to))
    return lax.ppermute(value, WHOLE, table)


def trade(value):
    return lax.ppermute(value, "core", [(0, 1), (1, 0)])


def extra(count, rows):
    return -(-count // rows)


def encode(block_of, count, out, largest_ref, place=()):
    rows = out.shape[-2]
    for at in range(count):
        largest_ref[at : at + 1] = jnp.max(jnp.abs(block_of(at)), axis=0, keepdims=True)
    if count % rows:
        largest_ref[count:] = jnp.zeros_like(largest_ref[count:])
    exponents = exponents_of(largest_ref[...])
    largest_ref[...] = jnp.exp2(exponents * (-1.0 / STEPS)) * FULL
    for at in range(count):
        codes = jnp.round(block_of(at) * largest_ref[at : at + 1])
        out[*place, at] = codes.astype(jnp.int32).astype(jnp.int16)
    for at in range(extra(count, rows)):
        out[*place, count + at] = exponent_codes(exponents[at * rows : (at + 1) * rows])


def scale_blocks(piece, count, place=()):
    rows = piece.shape[-2]
    blocks = [scales_of(piece[*place, count + at]) for at in range(extra(count, rows))]
    return [blocks[at // rows][at % rows : at % rows + 1] for at in range(count)]


def pack_kernel(place_ref, want_ref, *refs):
    gathered, outs = refs[:XS], refs[XS:]
    core = place_ref[2]
    for side in range(CORES):
        for far in range(XS):
            row = far * CORES + side
            for near in range(XS):
                slot = (near + core * (far - near)) * ZS
                for z in range(ZS):
                    outs[side * XS + far][near * ZS + z] = gathered[near][z, want_ref[row, slot + z]]


def contract_kernel(slot_ref, place_ref, *refs):
    pieces, block_ref, outs = refs[: 2 * XS], refs[2 * XS], refs[2 * XS + 1 : 4 * XS + 1]
    amp, total, largest = refs[4 * XS + 1 :]
    step = pl.program_id(0)
    _, slots, rows, half = total.shape
    part = rows // YS
    chunks = half // LANES

    def spot(side, far, near):
        core = place_ref[2] ^ side
        slot = pl.multiple_of((near + core * (far - near)) * ZS, ZS)
        return core, slot, pl.multiple_of((far + core * (near - far)) * part, part)

    @pl.when(step == 0)
    def _():
        for side in range(CORES):
            for far in range(XS):
                for near in range(XS):
                    at, slot, row = spot(side, far, near)
                    piece = pieces[side * XS + far][near * ZS : (near + 1) * ZS]
                    amp[at, pl.ds(slot, ZS), pl.ds(row, part)] = piece
        total[...] = jnp.zeros_like(total)

    def amplitudes(slot):
        return jnp.concatenate([amp[0, slot], amp[1, slot]], axis=1)

    for at in range(block_ref.shape[0]):
        task = step * block_ref.shape[0] + at
        first = slot_ref[2 * task]
        second = slot_ref[2 * task + 1]
        block = block_ref[at]
        term = lax.dot_general(
            amplitudes(second), block, (((1,), (1,)), ((), ())), preferred_element_type=jnp.float32
        )
        total[0, first] += term[:, :half]
        total[1, first] += term[:, half:]
        term = jnp.dot(amplitudes(first), block, preferred_element_type=jnp.float32)
        total[0, second] += term[:, :half]
        total[1, second] += term[:, half:]

    @pl.when(step == pl.num_programs(0) - 1)
    def _():
        for side in range(CORES):
            for far in range(XS):
                spots = [spot(side, far, near) for near in range(XS)]

                def block_of(block):
                    entry, lanes = block // chunks, block % chunks * LANES
                    at, slot, row = spots[entry // ZS]
                    return total[at, slot + entry % ZS, pl.ds(row, part), lanes : lanes + LANES]

                piece = side * XS + far
                encode(block_of, slots * chunks, outs[piece], largest.at[piece])


def contract(slots, place, pieces, blocks):
    entries, part, half = pieces[0].shape
    tasks, width, _ = blocks.shape
    count = entries * (half // LANES)
    out = (count + extra(count, part), part, LANES)
    halves = (CORES, entries, YS * part, half)
    return pl.pallas_call(
        contract_kernel,
        out_shape=[jax.ShapeDtypeStruct(out, jnp.int16)] * (2 * XS),
        grid_spec=pltpu.PrefetchScalarGridSpec(
            num_scalar_prefetch=2,
            grid=(tasks // PER_STEP,),
            in_specs=[VMEM] * (2 * XS)
            + [pl.BlockSpec((PER_STEP, width, width), lambda t, *_: (t, 0, 0))],
            out_specs=[VMEM] * (2 * XS),
            scratch_shapes=[
                pltpu.VMEM(halves, blocks.dtype),
                pltpu.VMEM(halves, jnp.float32),
                pltpu.VMEM((2 * XS, extra(count, part) * part, LANES), jnp.float32),
            ],
        ),
        compiler_params=pltpu.CompilerParams(vmem_limit_bytes=40 * MIB),
    )(slots, place, *pieces, blocks)


def combine_kernel(place_ref, want_ref, *refs):
    pieces, outs, totals, largest = refs[: 2 * XS], refs[2 * XS : 3 * XS], refs[3 * XS : -1], refs[-1]
    core = place_ref[2]
    tiles, rows, half = totals[0].shape
    per_owner = tiles // ZS
    chunks = half // LANES
    for total in totals:
        total[...] = jnp.zeros_like(total)
    for side in range(CORES):
        for far in range(XS):
            piece = pieces[side * XS + far]
            row = far * CORES + side
            scales = scale_blocks(piece, XS * ZS * chunks)
            for z in range(ZS):
                for near, total in enumerate(totals):
                    slot = (near + core * (far - near)) * ZS
                    tile = z * per_owner + want_ref[row, slot + z]
                    for chunk in range(chunks):
                        at = (near * ZS + z) * chunks + chunk
                        lanes = slice(chunk * LANES, (chunk + 1) * LANES)
                        total[tile, :, lanes] += numbers(piece[at]) * scales[at]
    for near, total in enumerate(totals):

        def block_of(at):
            return total[at // chunks, :, at % chunks * LANES : (at % chunks + 1) * LANES]

        encode(block_of, tiles * chunks, outs[near], largest.at[near])


def regroup_kernel(*refs):
    pieces, out, largest = refs[:XS], refs[XS], refs[XS + 1]
    rows = out.shape[2]
    count = out.shape[1] - largest.shape[1] // rows
    scales = [scale_blocks(piece, ZS * count) for piece in pieces]
    for z in range(ZS):
        sums = []
        for at in range(z * count, (z + 1) * count):
            sums.append(sum(numbers(piece[at]) * scale[at] for piece, scale in zip(pieces, scales)))
        encode(lambda at: sums[at], count, out, largest.at[z], (z,))


def finish_kernel(place_ref, pieces, keep, send):
    per_owner, rows, half = keep.shape
    chunks = half // LANES
    mine = pl.multiple_of(place_ref[2] * rows, rows)
    scales = [scale_blocks(pieces, per_owner * chunks, (z,)) for z in range(ZS)]
    for out, row in ((keep, mine), (send, rows - mine)):
        row = pl.multiple_of(row, rows)
        for which in range(per_owner):
            for chunk in range(chunks):
                at = which * chunks + chunk
                found = sum(numbers(pieces[z, at, pl.ds(row, rows)]) * scales[z][at] for z in range(ZS))
                out[which, :, chunk * LANES : (chunk + 1) * LANES] = found


def local(amplitudes, tasks, integrals):
    rows, per_owner, width = amplitudes.shape
    half = width // 2
    entries = XS * ZS
    part = CORES * rows
    kind = amplitudes.dtype
    place = jnp.stack([lax.axis_index(axis) for axis in PLANE]).astype(jnp.int32)
    x, core = place[0], place[2]

    def in_order(own, other, axis):
        found = jnp.concatenate([own, other], axis=axis)
        return jnp.where(core == 0, found, jnp.concatenate([other, own], axis=axis))

    tiles = amplitudes.transpose(1, 0, 2)
    low, high = tiles[..., :half], tiles[..., half:]
    own, other = jnp.where(core == 0, low, high), jnp.where(core == 0, high, low)
    tiles = in_order(own, trade(other), 1)
    along_z = swap(jnp.broadcast_to(tiles[None], (ZS, *tiles.shape)), "z")
    gathered = [along_z] + [move(along_z, near, True) for near in range(1, XS)]

    names = tasks.reshape(-1)
    owner = names * 171 >> 9
    slots = ((x - (owner // ZS)) & (XS - 1)) * ZS + (owner & (ZS - 1))
    lane = lax.broadcasted_iota(jnp.int32, (names.shape[0], LANES), 1)
    which = (names - owner * per_owner)[:, None]
    want = jnp.max(jnp.where(slots[:, None] == lane, which, 0), axis=0, keepdims=True)
    want = jnp.concatenate([want, trade(want)])
    wants = jnp.concatenate([want] + [move(want, -far, False) for far in range(1, XS)])

    piece = jax.ShapeDtypeStruct((entries, part, half), kind)
    packed = call(pack_kernel, [piece] * (2 * XS), [SMEM] * 2 + [VMEM] * XS)(place, wants, *gathered)
    direct, via = packed[:XS], packed[XS:]
    via = [trade(v) if far == 0 else move(v, far, False, 1) for far, v in enumerate(via)]
    direct = [v if far == 0 else move(v, far, False) for far, v in enumerate(direct)]

    codes = contract(slots, place, direct + via, integrals)

    via = [trade(v) if far == 0 else move(v, -far, True, 1) for far, v in enumerate(codes[XS:])]
    direct = [v if far == 0 else move(v, -far, False) for far, v in enumerate(codes[:XS])]
    tiles = ZS * per_owner
    chunks = half // LANES
    count = tiles * chunks
    cut = jax.ShapeDtypeStruct((count + extra(count, part), part, LANES), jnp.int16)
    by_near = call(
        combine_kernel,
        [cut] * XS,
        [SMEM] * 2 + [VMEM] * (2 * XS),
        [pltpu.VMEM((tiles, part, half), jnp.float32)] * XS
        + [pltpu.VMEM((XS, extra(count, part) * part, LANES), jnp.float32)],
    )(place, wants, *direct, *via)
    by_near = [v if near == 0 else move(v, -near, True) for near, v in enumerate(by_near)]
    count = per_owner * chunks
    cut = jax.ShapeDtypeStruct((ZS, count + extra(count, part), part, LANES), jnp.int16)
    largest = pltpu.VMEM((ZS, extra(count, part) * part, LANES), jnp.float32)
    by_z = swap(call(regroup_kernel, cut, [VMEM] * XS, [largest])(*by_near), "z")
    out = jax.ShapeDtypeStruct((per_owner, rows, half), jnp.float32)
    keep, send = call(finish_kernel, [out] * 2, [SMEM, VMEM])(place, by_z)
    return in_order(keep, trade(send), 2).transpose(1, 0, 2)


def solution(mesh):
    fine = Mesh(mesh.devices.reshape(XS, ZS, YS, CORES), ("x", "z", "y", "core"))
    tile, pair = ("x", "z"), ("y", "core")
    return jax.shard_map(
        local,
        mesh=fine,
        in_specs=(P(pair, tile, None), P(tile + pair, None), P(tile + pair, None, None)),
        out_specs=P(pair, tile, None),
        check_vma=False,
    )
```

```python
import functools

import jax
import jax.numpy as jnp
from jax import lax
from jax.experimental import pallas as pl
from jax.experimental.pallas import tpu as pltpu
from jax.sharding import Mesh
from jax.sharding import PartitionSpec as P

XS, ZS, YS, CORES = 4, 8, 4, 2
PLANE = ("x", "y", "core")
WHOLE = ("x", "z", "y", "core")
PER_STEP = 8
LIMIT = 32

LANES = 128
FULL = 32767.0
STEPS = 256.0
FLOOR = 2.0**-110
MIB = 1024 * 1024
VMEM = pl.BlockSpec(memory_space=pltpu.VMEM)
SMEM = pl.BlockSpec(memory_space=pltpu.SMEM)


def swap(value, axes):
    return lax.all_to_all(value, axes, split_axis=0, concat_axis=0, tiled=True)


def exponents_of(largest):
    return jnp.ceil(jnp.log2(jnp.maximum(largest, FLOOR)) * STEPS)


def exponent_codes(exponents):
    return exponents.astype(jnp.int32).astype(jnp.int16)


def numbers(codes):
    return codes.astype(jnp.int32).astype(jnp.float32)


def scales_of(codes):
    return jnp.exp2(numbers(codes) * (1.0 / STEPS)) * (1.0 / FULL)


def call(kernel, out_shape, in_specs, scratch=()):
    return pl.pallas_call(
        kernel,
        out_shape=out_shape,
        in_specs=in_specs,
        out_specs=jax.tree.map(lambda _: VMEM, out_shape),
        scratch_shapes=scratch,
        compiler_params=pltpu.CompilerParams(vmem_limit_bytes=24 * MIB),
    )


def device(x, z, y, core):
    return ((x % XS * ZS + z) * YS + y % YS) * CORES + core


def move(value, by, near, cross=0):
    table = []
    for x in range(XS):
        for z in range(ZS):
            for y in range(YS):
                for core in range(CORES):
                    along_x = (core == 0) == near
                    to = device(x + by * along_x, z, y + by * (not along_x), core ^ cross)
                    table.append((device(x, z, y, core), to))
    return lax.ppermute(value, WHOLE, table)


def trade(value):
    return lax.ppermute(value, "core", [(0, 1), (1, 0)])


def extra(count, rows):
    return -(-count // rows)


def encode(block_of, count, out, largest_ref, place=()):
    rows = out.shape[-2]
    for at in range(count):
        largest_ref[at : at + 1] = jnp.max(jnp.abs(block_of(at)), axis=0, keepdims=True)
    if count % rows:
        largest_ref[count:] = jnp.zeros_like(largest_ref[count:])
    exponents = exponents_of(largest_ref[...])
    largest_ref[...] = jnp.exp2(exponents * (-1.0 / STEPS)) * FULL
    for at in range(count):
        codes = jnp.round(block_of(at) * largest_ref[at : at + 1])
        out[*place, at] = codes.astype(jnp.int32).astype(jnp.int16)
    for at in range(extra(count, rows)):
        out[*place, count + at] = exponent_codes(exponents[at * rows : (at + 1) * rows])


def scale_blocks(piece, count, place=()):
    rows = piece.shape[-2]
    blocks = [scales_of(piece[*place, count + at]) for at in range(extra(count, rows))]
    return [blocks[at // rows][at % rows : at % rows + 1] for at in range(count)]


def pack_kernel(place_ref, want_ref, *refs):
    gathered, outs = refs[:XS], refs[XS:]
    core = place_ref[2]
    for side in range(CORES):
        for far in range(XS):
            row = far * CORES + side
            for near in range(XS):
                slot = (near + core * (far - near)) * ZS
                for z in range(ZS):
                    outs[side * XS + far][near * ZS + z] = gathered[near][z, want_ref[row, slot + z]]


def spot(place_ref, side, far, near, part):
    core = place_ref[2] ^ side
    slot = pl.multiple_of((near + core * (far - near)) * ZS, ZS)
    return slot, pl.multiple_of((far + core * (near - far)) * part, part)


def lay_out(place_ref, side, pieces, amp):
    part = pieces[0].shape[1]
    for far, piece in enumerate(pieces):
        for near in range(XS):
            slot, row = spot(place_ref, side, far, near, part)
            amp[pl.ds(slot, ZS), pl.ds(row, part)] = piece[near * ZS : (near + 1) * ZS]


def begin_kernel(slot_ref, place_ref, *refs):
    pieces, (across_ref, along_ref, total, amp) = refs[:XS], refs[XS:]
    step = pl.program_id(0)
    half = amp.shape[2]

    @pl.when(step == 0)
    def _():
        lay_out(place_ref, 0, pieces, amp)
        total[...] = jnp.zeros_like(total)

    for at in range(along_ref.shape[0]):
        task = step * along_ref.shape[0] + at
        first = slot_ref[2 * task]
        second = slot_ref[2 * task + 1]
        term = lax.dot_general(
            amp[second], across_ref[at], (((1,), (1,)), ((), ())), preferred_element_type=jnp.float32
        )
        total[0, first] += term[:, :half]
        total[1, first] += term[:, half:]
        term = jnp.dot(amp[first], along_ref[at], preferred_element_type=jnp.float32)
        total[0, second] += term[:, :half]
        total[1, second] += term[:, half:]


def end_kernel(side, slot_ref, place_ref, *refs):
    pieces, (begun, first_ref, second_ref), refs = refs[:XS], refs[XS : XS + 3], refs[XS + 3 :]
    outs, (amp, total, largest) = refs[:XS], refs[XS:]
    step = pl.program_id(0)
    slots, rows, half = total.shape
    part = rows // YS
    chunks = half // LANES

    @pl.when(step == 0)
    def _():
        lay_out(place_ref, 1, pieces, amp)
        total[...] = begun[place_ref[2] ^ side]

    for at in range(first_ref.shape[0]):
        task = step * first_ref.shape[0] + at
        first = slot_ref[2 * task]
        second = slot_ref[2 * task + 1]
        total[first] += lax.dot_general(
            amp[second], first_ref[at], (((1,), (1,)), ((), ())), preferred_element_type=jnp.float32
        )
        total[second] += jnp.dot(amp[first], second_ref[at], preferred_element_type=jnp.float32)

    @pl.when(step == pl.num_programs(0) - 1)
    def _():
        for far in range(XS):
            spots = [spot(place_ref, side, far, near, part) for near in range(XS)]

            def block_of(block):
                entry, lanes = block // chunks, block % chunks * LANES
                slot, row = spots[entry // ZS]
                return total[slot + entry % ZS, pl.ds(row, part), lanes : lanes + LANES]

            encode(block_of, slots * chunks, outs[far], largest.at[far])


def products(kernel, slots, place, operands, blocks, specs, out_shape, scratch, share):
    tasks, width, _ = blocks.shape
    return pl.pallas_call(
        kernel,
        out_shape=out_shape,
        grid_spec=pltpu.PrefetchScalarGridSpec(
            num_scalar_prefetch=2,
            grid=(tasks // PER_STEP,),
            in_specs=[VMEM] * len(operands) + specs,
            out_specs=jax.tree.map(lambda _: VMEM, out_shape),
            scratch_shapes=scratch,
        ),
        compiler_params=pltpu.CompilerParams(vmem_limit_bytes=LIMIT * MIB),
        cost_estimate=pl.CostEstimate(
            flops=4 * tasks * 128 * width * width // share,
            bytes_accessed=4 * tasks * width * width // share,
            transcendentals=0,
        ),
    )(slots, place, *operands, blocks, blocks)


def begin(slots, place, pieces, blocks):
    entries, part, half = pieces[0].shape
    width = blocks.shape[1]
    specs = [
        pl.BlockSpec((PER_STEP, width, half), lambda t, _, place: (t, 0, place[2])),
        pl.BlockSpec((PER_STEP, half, width), lambda t, _, place: (t, place[2], 0)),
    ]
    out = jax.ShapeDtypeStruct((CORES, entries, YS * part, half), jnp.float32)
    scratch = [pltpu.VMEM((entries, YS * part, half), blocks.dtype)]
    return products(begin_kernel, slots, place, pieces, blocks, specs, out, scratch, 2)


def end(side, slots, place, pieces, begun, blocks):
    entries, part, half = pieces[0].shape
    specs = [
        pl.BlockSpec((PER_STEP, half, half), lambda t, _, place: (t, place[2] ^ side, 1 - place[2])),
        pl.BlockSpec((PER_STEP, half, half), lambda t, _, place: (t, 1 - place[2], place[2] ^ side)),
    ]
    count = entries * (half // LANES)
    out = jax.ShapeDtypeStruct((count + extra(count, part), part, LANES), jnp.int16)
    scratch = [
        pltpu.VMEM((entries, YS * part, half), blocks.dtype),
        pltpu.VMEM((entries, YS * part, half), jnp.float32),
        pltpu.VMEM((XS, extra(count, part) * part, LANES), jnp.float32),
    ]
    operands = [*pieces, begun]
    kernel = functools.partial(end_kernel, side)
    return products(kernel, slots, place, operands, blocks, specs, [out] * XS, scratch, 4)


def combine_kernel(place_ref, want_ref, *refs):
    pieces, outs, totals, largest = refs[: 2 * XS], refs[2 * XS : 3 * XS], refs[3 * XS : -1], refs[-1]
    core = place_ref[2]
    tiles, rows, half = totals[0].shape
    per_owner = tiles // ZS
    chunks = half // LANES
    for total in totals:
        total[...] = jnp.zeros_like(total)
    for side in range(CORES):
        for far in range(XS):
            piece = pieces[side * XS + far]
            row = far * CORES + side
            scales = scale_blocks(piece, XS * ZS * chunks)
            for z in range(ZS):
                for near, total in enumerate(totals):
                    slot = (near + core * (far - near)) * ZS
                    tile = z * per_owner + want_ref[row, slot + z]
                    for chunk in range(chunks):
                        at = (near * ZS + z) * chunks + chunk
                        lanes = slice(chunk * LANES, (chunk + 1) * LANES)
                        total[tile, :, lanes] += numbers(piece[at]) * scales[at]
    for near, total in enumerate(totals):

        def block_of(at):
            return total[at // chunks, :, at % chunks * LANES : (at % chunks + 1) * LANES]

        encode(block_of, tiles * chunks, outs[near], largest.at[near])


def regroup_kernel(*refs):
    pieces, out, largest = refs[:XS], refs[XS], refs[XS + 1]
    rows = out.shape[2]
    count = out.shape[1] - largest.shape[1] // rows
    scales = [scale_blocks(piece, ZS * count) for piece in pieces]
    for z in range(ZS):
        sums = []
        for at in range(z * count, (z + 1) * count):
            sums.append(sum(numbers(piece[at]) * scale[at] for piece, scale in zip(pieces, scales)))
        encode(lambda at: sums[at], count, out, largest.at[z], (z,))


def finish_kernel(place_ref, pieces, keep, send):
    per_owner, rows, half = keep.shape
    chunks = half // LANES
    mine = pl.multiple_of(place_ref[2] * rows, rows)
    scales = [scale_blocks(pieces, per_owner * chunks, (z,)) for z in range(ZS)]
    for out, row in ((keep, mine), (send, rows - mine)):
        row = pl.multiple_of(row, rows)
        for which in range(per_owner):
            for chunk in range(chunks):
                at = which * chunks + chunk
                found = sum(numbers(pieces[z, at, pl.ds(row, rows)]) * scales[z][at] for z in range(ZS))
                out[which, :, chunk * LANES : (chunk + 1) * LANES] = found


def local(amplitudes, tasks, integrals):
    rows, per_owner, width = amplitudes.shape
    half = width // 2
    entries = XS * ZS
    part = CORES * rows
    kind = amplitudes.dtype
    place = jnp.stack([lax.axis_index(axis) for axis in PLANE]).astype(jnp.int32)
    x, core = place[0], place[2]

    def in_order(own, other, axis):
        found = jnp.concatenate([own, other], axis=axis)
        return jnp.where(core == 0, found, jnp.concatenate([other, own], axis=axis))

    tiles = amplitudes.transpose(1, 0, 2)
    low, high = tiles[..., :half], tiles[..., half:]
    own, other = jnp.where(core == 0, low, high), jnp.where(core == 0, high, low)
    tiles = in_order(own, trade(other), 1)
    along_z = swap(jnp.broadcast_to(tiles[None], (ZS, *tiles.shape)), "z")
    gathered = [along_z] + [move(along_z, near, True) for near in range(1, XS)]

    names = tasks.reshape(-1)
    owner = names * 171 >> 9
    slots = ((x - (owner // ZS)) & (XS - 1)) * ZS + (owner & (ZS - 1))
    lane = lax.broadcasted_iota(jnp.int32, (names.shape[0], LANES), 1)
    which = (names - owner * per_owner)[:, None]
    want = jnp.max(jnp.where(slots[:, None] == lane, which, 0), axis=0, keepdims=True)
    want = jnp.concatenate([want, trade(want)])
    wants = jnp.concatenate([want] + [move(want, -far, False) for far in range(1, XS)])

    piece = jax.ShapeDtypeStruct((entries, part, half), kind)
    packed = call(pack_kernel, [piece] * (2 * XS), [SMEM] * 2 + [VMEM] * XS)(place, wants, *gathered)
    direct, via = packed[:XS], packed[XS:]
    via = [trade(v) if far == 0 else move(v, far, False, 1) for far, v in enumerate(via)]
    direct = [v if far == 0 else move(v, far, False) for far, v in enumerate(direct)]

    begun = begin(slots, place, direct, integrals)
    codes = end(0, slots, place, via, begun, integrals)
    onward = end(1, slots, place, via, begun, integrals)
    direct = [v if far == 0 else move(v, -far, False) for far, v in enumerate(codes)]
    via = [trade(v) if far == 0 else move(v, -far, True, 1) for far, v in enumerate(onward)]
    tiles = ZS * per_owner
    chunks = half // LANES
    count = tiles * chunks
    cut = jax.ShapeDtypeStruct((count + extra(count, part), part, LANES), jnp.int16)
    by_near = call(
        combine_kernel,
        [cut] * XS,
        [SMEM] * 2 + [VMEM] * (2 * XS),
        [pltpu.VMEM((tiles, part, half), jnp.float32)] * XS
        + [pltpu.VMEM((XS, extra(count, part) * part, LANES), jnp.float32)],
    )(place, wants, *direct, *via)
    by_near = [v if near == 0 else move(v, -near, True) for near, v in enumerate(by_near)]
    count = per_owner * chunks
    cut = jax.ShapeDtypeStruct((ZS, count + extra(count, part), part, LANES), jnp.int16)
    largest = pltpu.VMEM((ZS, extra(count, part) * part, LANES), jnp.float32)
    by_z = swap(call(regroup_kernel, cut, [VMEM] * XS, [largest])(*by_near), "z")
    out = jax.ShapeDtypeStruct((per_owner, rows, half), jnp.float32)
    keep, send = call(finish_kernel, [out] * 2, [SMEM, VMEM])(place, by_z)
    return in_order(keep, trade(send), 2).transpose(1, 0, 2)


def solution(mesh):
    fine = Mesh(mesh.devices.reshape(XS, ZS, YS, CORES), ("x", "z", "y", "core"))
    tile, pair = ("x", "z"), ("y", "core")
    return jax.shard_map(
        local,
        mesh=fine,
        in_specs=(P(pair, tile, None), P(tile + pair, None), P(tile + pair, None, None)),
        out_specs=P(pair, tile, None),
        check_vma=False,
    )
```

```python
import functools

import jax
import jax.numpy as jnp
from jax import lax
from jax.experimental import pallas as pl
from jax.experimental.pallas import tpu as pltpu
from jax.sharding import Mesh
from jax.sharding import PartitionSpec as P

XS, ZS, YS, CORES = 4, 8, 4, 2
PLANE = ("x", "y", "core")
WHOLE = ("x", "z", "y", "core")
PER_STEP = 12
LIMIT = 32

LANES = 128
FULL = 32767.0
STEPS = 256.0
FLOOR = 2.0**-110
MIB = 1024 * 1024
VMEM = pl.BlockSpec(memory_space=pltpu.VMEM)
SMEM = pl.BlockSpec(memory_space=pltpu.SMEM)


def swap(value, axes):
    return lax.all_to_all(value, axes, split_axis=0, concat_axis=0, tiled=True)


def exponents_of(largest):
    return jnp.ceil(jnp.log2(jnp.maximum(largest, FLOOR)) * STEPS)


def exponent_codes(exponents):
    return exponents.astype(jnp.int32).astype(jnp.int16)


def numbers(codes):
    return codes.astype(jnp.int32).astype(jnp.float32)


def scales_of(codes):
    return jnp.exp2(numbers(codes) * (1.0 / STEPS)) * (1.0 / FULL)


def call(kernel, out_shape, in_specs, scratch=()):
    return pl.pallas_call(
        kernel,
        out_shape=out_shape,
        in_specs=in_specs,
        out_specs=jax.tree.map(lambda _: VMEM, out_shape),
        scratch_shapes=scratch,
        compiler_params=pltpu.CompilerParams(vmem_limit_bytes=24 * MIB),
    )


def device(x, z, y, core):
    return ((x % XS * ZS + z) * YS + y % YS) * CORES + core


def move(value, by, near, cross=0):
    table = []
    for x in range(XS):
        for z in range(ZS):
            for y in range(YS):
                for core in range(CORES):
                    along_x = (core == 0) == near
                    to = device(x + by * along_x, z, y + by * (not along_x), core ^ cross)
                    table.append((device(x, z, y, core), to))
    return lax.ppermute(value, WHOLE, table)


def trade(value):
    return lax.ppermute(value, "core", [(0, 1), (1, 0)])


def extra(count, rows):
    return -(-count // rows)


def encode(block_of, count, out, largest_ref, place=()):
    rows = out.shape[-2]
    for at in range(count):
        largest_ref[at : at + 1] = jnp.max(jnp.abs(block_of(at)), axis=0, keepdims=True)
    if count % rows:
        largest_ref[count:] = jnp.zeros_like(largest_ref[count:])
    exponents = exponents_of(largest_ref[...])
    largest_ref[...] = jnp.exp2(exponents * (-1.0 / STEPS)) * FULL
    for at in range(count):
        codes = jnp.round(block_of(at) * largest_ref[at : at + 1])
        out[*place, at] = codes.astype(jnp.int32).astype(jnp.int16)
    for at in range(extra(count, rows)):
        out[*place, count + at] = exponent_codes(exponents[at * rows : (at + 1) * rows])


def scale_blocks(piece, count, place=()):
    rows = piece.shape[-2]
    blocks = [scales_of(piece[*place, count + at]) for at in range(extra(count, rows))]
    return [blocks[at // rows][at % rows : at % rows + 1] for at in range(count)]


def pack_kernel(place_ref, want_ref, *refs):
    gathered, outs = refs[:XS], refs[XS:]
    core = place_ref[2]
    for side in range(CORES):
        for far in range(XS):
            row = far * CORES + side
            for near in range(XS):
                slot = (near + core * (far - near)) * ZS
                for z in range(ZS):
                    which = want_ref[row, slot + z]
                    for part in range(CORES):
                        found = gathered[near][z * CORES + part, which]
                        rows = slice(part * found.shape[0], (part + 1) * found.shape[0])
                        outs[side * XS + far][near * ZS + z, rows] = found


def spot(place_ref, side, far, near, part):
    core = place_ref[2] ^ side
    slot = pl.multiple_of((near + core * (far - near)) * ZS, ZS)
    return slot, pl.multiple_of((far + core * (near - far)) * part, part)


def lay_out(place_ref, side, pieces, amp):
    part = pieces[0].shape[1]
    for far, piece in enumerate(pieces):
        for near in range(XS):
            slot, row = spot(place_ref, side, far, near, part)
            amp[pl.ds(slot, ZS), pl.ds(row, part)] = piece[near * ZS : (near + 1) * ZS]


def begin_kernel(slot_ref, place_ref, *refs):
    pieces, (across_ref, along_ref, total, amp) = refs[:XS], refs[XS:]
    step = pl.program_id(0)
    half = amp.shape[2]

    @pl.when(step == 0)
    def _():
        lay_out(place_ref, 0, pieces, amp)
        total[...] = jnp.zeros_like(total)

    for at in range(along_ref.shape[0]):
        task = step * along_ref.shape[0] + at
        first = slot_ref[2 * task]
        second = slot_ref[2 * task + 1]
        term = lax.dot_general(
            amp[second], across_ref[at], (((1,), (1,)), ((), ())), preferred_element_type=jnp.float32
        )
        total[0, first] += term[:, :half]
        total[1, first] += term[:, half:]
        term = jnp.dot(amp[first], along_ref[at], preferred_element_type=jnp.float32)
        total[0, second] += term[:, :half]
        total[1, second] += term[:, half:]


def end_kernel(side, slot_ref, place_ref, *refs):
    pieces, (begun, first_ref, second_ref), refs = refs[:XS], refs[XS : XS + 3], refs[XS + 3 :]
    outs, (amp, total, largest) = refs[:XS], refs[XS:]
    step = pl.program_id(0)
    slots, rows, half = total.shape
    part = rows // YS
    chunks = half // LANES

    @pl.when(step == 0)
    def _():
        lay_out(place_ref, 1, pieces, amp)
        total[...] = begun[place_ref[2] ^ side]

    for at in range(first_ref.shape[0]):
        task = step * first_ref.shape[0] + at
        first = slot_ref[2 * task]
        second = slot_ref[2 * task + 1]
        total[first] += lax.dot_general(
            amp[second], first_ref[at], (((1,), (1,)), ((), ())), preferred_element_type=jnp.float32
        )
        total[second] += jnp.dot(amp[first], second_ref[at], preferred_element_type=jnp.float32)

    @pl.when(step == pl.num_programs(0) - 1)
    def _():
        for far in range(XS):
            spots = [spot(place_ref, side, far, near, part) for near in range(XS)]

            def block_of(block):
                entry, lanes = block // chunks, block % chunks * LANES
                slot, row = spots[entry // ZS]
                return total[slot + entry % ZS, pl.ds(row, part), lanes : lanes + LANES]

            encode(block_of, slots * chunks, outs[far], largest.at[far])


def products(kernel, slots, place, operands, blocks, specs, out_shape, scratch, share):
    tasks, width, _ = blocks.shape
    return pl.pallas_call(
        kernel,
        out_shape=out_shape,
        grid_spec=pltpu.PrefetchScalarGridSpec(
            num_scalar_prefetch=2,
            grid=(tasks // PER_STEP,),
            in_specs=[VMEM] * len(operands) + specs,
            out_specs=jax.tree.map(lambda _: VMEM, out_shape),
            scratch_shapes=scratch,
        ),
        compiler_params=pltpu.CompilerParams(vmem_limit_bytes=LIMIT * MIB),
        cost_estimate=pl.CostEstimate(
            flops=4 * tasks * 128 * width * width // share,
            bytes_accessed=4 * tasks * width * width // share,
            transcendentals=0,
        ),
    )(slots, place, *operands, blocks, blocks)


def begin(slots, place, pieces, blocks):
    entries, part, half = pieces[0].shape
    width = blocks.shape[1]
    specs = [
        pl.BlockSpec((PER_STEP, width, half), lambda t, _, place: (t, 0, place[2])),
        pl.BlockSpec((PER_STEP, half, width), lambda t, _, place: (t, place[2], 0)),
    ]
    out = jax.ShapeDtypeStruct((CORES, entries, YS * part, half), jnp.float32)
    scratch = [pltpu.VMEM((entries, YS * part, half), blocks.dtype)]
    return products(begin_kernel, slots, place, pieces, blocks, specs, out, scratch, 2)


def end(side, slots, place, pieces, begun, blocks):
    entries, part, half = pieces[0].shape
    specs = [
        pl.BlockSpec((PER_STEP, half, half), lambda t, _, place: (t, place[2] ^ side, 1 - place[2])),
        pl.BlockSpec((PER_STEP, half, half), lambda t, _, place: (t, 1 - place[2], place[2] ^ side)),
    ]
    count = entries * (half // LANES)
    out = jax.ShapeDtypeStruct((count + extra(count, part), part, LANES), jnp.int16)
    scratch = [
        pltpu.VMEM((entries, YS * part, half), blocks.dtype),
        pltpu.VMEM((entries, YS * part, half), jnp.float32),
        pltpu.VMEM((XS, extra(count, part) * part, LANES), jnp.float32),
    ]
    operands = [*pieces, begun]
    kernel = functools.partial(end_kernel, side)
    return products(kernel, slots, place, operands, blocks, specs, [out] * XS, scratch, 4)


def combine_kernel(place_ref, want_ref, *refs):
    pieces, outs, totals, largest = refs[: 2 * XS], refs[2 * XS : 3 * XS], refs[3 * XS : -1], refs[-1]
    core = place_ref[2]
    tiles, rows, half = totals[0].shape
    per_owner = tiles // ZS
    chunks = half // LANES
    for total in totals:
        total[...] = jnp.zeros_like(total)
    for side in range(CORES):
        for far in range(XS):
            piece = pieces[side * XS + far]
            row = far * CORES + side
            scales = scale_blocks(piece, XS * ZS * chunks)
            for z in range(ZS):
                for near, total in enumerate(totals):
                    slot = (near + core * (far - near)) * ZS
                    tile = z * per_owner + want_ref[row, slot + z]
                    for chunk in range(chunks):
                        at = (near * ZS + z) * chunks + chunk
                        lanes = slice(chunk * LANES, (chunk + 1) * LANES)
                        total[tile, :, lanes] += numbers(piece[at]) * scales[at]
    for near, total in enumerate(totals):

        def block_of(at):
            return total[at // chunks, :, at % chunks * LANES : (at % chunks + 1) * LANES]

        encode(block_of, tiles * chunks, outs[near], largest.at[near])


def regroup_kernel(*refs):
    pieces, out, largest = refs[:XS], refs[XS], refs[XS + 1]
    rows = out.shape[2]
    count = out.shape[1] - extra(out.shape[1] - 1, rows)
    scales = [scale_blocks(piece, ZS * count) for piece in pieces]
    for z in range(ZS):
        sums = []
        for at in range(z * count, (z + 1) * count):
            sums.append(sum(numbers(piece[at]) * scale[at] for piece, scale in zip(pieces, scales)))
        for core in range(CORES):
            to = z * CORES + core
            encode(lambda at: sums[at][core * rows : (core + 1) * rows], count, out, largest.at[to], (to,))


def finish_kernel(pieces, out):
    per_owner, _, width = out.shape
    chunks = width // CORES // LANES
    scales = [scale_blocks(pieces, per_owner * chunks, (source,)) for source in range(ZS * CORES)]
    for core in range(CORES):
        for which in range(per_owner):
            for chunk in range(chunks):
                at = which * chunks + chunk
                sources = [z * CORES + core for z in range(ZS)]
                found = sum(numbers(pieces[source, at]) * scales[source][at] for source in sources)
                lane = (core * chunks + chunk) * LANES
                out[which, :, lane : lane + LANES] = found


def local(amplitudes, tasks, integrals):
    rows, per_owner, width = amplitudes.shape
    half = width // 2
    entries = XS * ZS
    part = CORES * rows
    kind = amplitudes.dtype
    place = jnp.stack([lax.axis_index(axis) for axis in PLANE]).astype(jnp.int32)
    x = place[0]

    tiles = amplitudes.transpose(1, 0, 2)
    halves = jnp.stack([tiles[..., :half], tiles[..., half:]])
    halves = jnp.broadcast_to(halves[None], (ZS, *halves.shape)).reshape(-1, *halves.shape[1:])
    along_z = swap(halves, ("z", "core"))
    gathered = [along_z] + [move(along_z, near, True) for near in range(1, XS)]

    names = tasks.reshape(-1)
    owner = names * 171 >> 9
    slots = ((x - (owner // ZS)) & (XS - 1)) * ZS + (owner & (ZS - 1))
    lane = lax.broadcasted_iota(jnp.int32, (names.shape[0], LANES), 1)
    which = (names - owner * per_owner)[:, None]
    want = jnp.max(jnp.where(slots[:, None] == lane, which, 0), axis=0, keepdims=True)
    want = jnp.concatenate([want, trade(want)])
    wants = jnp.concatenate([want] + [move(want, -far, False) for far in range(1, XS)])

    piece = jax.ShapeDtypeStruct((entries, part, half), kind)
    packed = call(pack_kernel, [piece] * (2 * XS), [SMEM] * 2 + [VMEM] * XS)(place, wants, *gathered)
    direct, via = packed[:XS], packed[XS:]
    via = [trade(v) if far == 0 else move(v, far, False, 1) for far, v in enumerate(via)]
    direct = [v if far == 0 else move(v, far, False) for far, v in enumerate(direct)]

    begun = begin(slots, place, direct, integrals)
    codes = end(0, slots, place, via, begun, integrals)
    onward = end(1, slots, place, via, begun, integrals)
    direct = [v if far == 0 else move(v, -far, False) for far, v in enumerate(codes)]
    via = [trade(v) if far == 0 else move(v, -far, True, 1) for far, v in enumerate(onward)]
    tiles = ZS * per_owner
    chunks = half // LANES
    count = tiles * chunks
    cut = jax.ShapeDtypeStruct((count + extra(count, part), part, LANES), jnp.int16)
    by_near = call(
        combine_kernel,
        [cut] * XS,
        [SMEM] * 2 + [VMEM] * (2 * XS),
        [pltpu.VMEM((tiles, part, half), jnp.float32)] * XS
        + [pltpu.VMEM((XS, extra(count, part) * part, LANES), jnp.float32)],
    )(place, wants, *direct, *via)
    by_near = [v if near == 0 else move(v, -near, True) for near, v in enumerate(by_near)]
    count = per_owner * chunks
    cut = jax.ShapeDtypeStruct((ZS * CORES, count + extra(count, rows), rows, LANES), jnp.int16)
    largest = pltpu.VMEM((ZS * CORES, extra(count, rows) * rows, LANES), jnp.float32)
    by_z = swap(call(regroup_kernel, cut, [VMEM] * XS, [largest])(*by_near), ("z", "core"))
    out = jax.ShapeDtypeStruct((per_owner, rows, width), jnp.float32)
    return call(finish_kernel, out, [VMEM])(by_z).transpose(1, 0, 2)


def solution(mesh):
    fine = Mesh(mesh.devices.reshape(XS, ZS, YS, CORES), ("x", "z", "y", "core"))
    tile, pair = ("x", "z"), ("y", "core")
    return jax.shard_map(
        local,
        mesh=fine,
        in_specs=(P(pair, tile, None), P(tile + pair, None), P(tile + pair, None, None)),
        out_specs=P(pair, tile, None),
        check_vma=False,
    )
```

```python
import functools

import jax
import jax.numpy as jnp
from jax import lax
from jax.experimental import pallas as pl
from jax.experimental.pallas import tpu as pltpu
from jax.sharding import Mesh
from jax.sharding import PartitionSpec as P

XS, ZS, YS, CORES = 4, 8, 4, 2
PLANE = ("x", "y", "core")
WHOLE = ("x", "z", "y", "core")
PER_STEP = 12
LIMIT = 32

LANES = 128
FULL = 32767.0
STEPS = 256.0
FLOOR = 2.0**-110
MIB = 1024 * 1024
VMEM = pl.BlockSpec(memory_space=pltpu.VMEM)
SMEM = pl.BlockSpec(memory_space=pltpu.SMEM)


def swap(value, axes):
    return lax.all_to_all(value, axes, split_axis=0, concat_axis=0, tiled=True)


def exponents_of(largest):
    return jnp.ceil(jnp.log2(jnp.maximum(largest, FLOOR)) * STEPS)


def exponent_codes(exponents):
    return exponents.astype(jnp.int32).astype(jnp.int16)


def numbers(codes):
    return codes.astype(jnp.int32).astype(jnp.float32)


def scales_of(codes):
    return jnp.exp2(numbers(codes) * (1.0 / STEPS)) * (1.0 / FULL)


def call(kernel, out_shape, in_specs, scratch=()):
    return pl.pallas_call(
        kernel,
        out_shape=out_shape,
        in_specs=in_specs,
        out_specs=jax.tree.map(lambda _: VMEM, out_shape),
        scratch_shapes=scratch,
        compiler_params=pltpu.CompilerParams(vmem_limit_bytes=24 * MIB),
    )


def device(x, z, y, core):
    return ((x % XS * ZS + z) * YS + y % YS) * CORES + core


def move(value, by, near, cross=0):
    table = []
    for x in range(XS):
        for z in range(ZS):
            for y in range(YS):
                for core in range(CORES):
                    along_x = (core == 0) == near
                    to = device(x + by * along_x, z, y + by * (not along_x), core ^ cross)
                    table.append((device(x, z, y, core), to))
    return lax.ppermute(value, WHOLE, table)


def trade(value):
    return lax.ppermute(value, "core", [(0, 1), (1, 0)])


def extra(count, rows):
    return -(-count // rows)


def encode(block_of, count, out, largest_ref, place=()):
    rows = out.shape[-2]
    for at in range(count):
        largest_ref[at : at + 1] = jnp.max(jnp.abs(block_of(at)), axis=0, keepdims=True)
    if count % rows:
        largest_ref[count:] = jnp.zeros_like(largest_ref[count:])
    exponents = exponents_of(largest_ref[...])
    largest_ref[...] = jnp.exp2(exponents * (-1.0 / STEPS)) * FULL
    for at in range(count):
        codes = jnp.round(block_of(at) * largest_ref[at : at + 1])
        out[*place, at] = codes.astype(jnp.int32).astype(jnp.int16)
    for at in range(extra(count, rows)):
        out[*place, count + at] = exponent_codes(exponents[at * rows : (at + 1) * rows])


def scale_blocks(piece, count, place=()):
    rows = piece.shape[-2]
    blocks = [scales_of(piece[*place, count + at]) for at in range(extra(count, rows))]
    return [blocks[at // rows][at % rows : at % rows + 1] for at in range(count)]


def pack_kernel(place_ref, want_ref, *refs):
    gathered, outs = refs[:XS], refs[XS:]
    core = place_ref[2]
    for side in range(CORES):
        for far in range(XS):
            row = far * CORES + side
            for near in range(XS):
                slot = (near + core * (far - near)) * ZS
                for z in range(ZS):
                    which = want_ref[row, slot + z]
                    for part in range(CORES):
                        found = gathered[near][z * CORES + part, which]
                        rows = slice(part * found.shape[0], (part + 1) * found.shape[0])
                        outs[side * XS + far][near * ZS + z, rows] = found


def spot(place_ref, side, far, near, part):
    core = place_ref[2] ^ side
    slot = pl.multiple_of((near + core * (far - near)) * ZS, ZS)
    return slot, pl.multiple_of((far + core * (near - far)) * part, part)


def lay_out(place_ref, side, pieces, amp):
    part = pieces[0].shape[1]
    for far, piece in enumerate(pieces):
        for near in range(XS):
            slot, row = spot(place_ref, side, far, near, part)
            amp[pl.ds(slot, ZS), pl.ds(row, part)] = piece[near * ZS : (near + 1) * ZS]


def begin_kernel(slot_ref, place_ref, *refs):
    pieces, (across_ref, along_ref, total, amp) = refs[:XS], refs[XS:]
    step = pl.program_id(0)
    half = amp.shape[2]

    @pl.when(step == 0)
    def _():
        lay_out(place_ref, 0, pieces, amp)
        total[...] = jnp.zeros_like(total)

    for at in range(along_ref.shape[0]):
        task = step * along_ref.shape[0] + at
        first = slot_ref[2 * task]
        second = slot_ref[2 * task + 1]
        term = lax.dot_general(
            amp[second], across_ref[at], (((1,), (1,)), ((), ())), preferred_element_type=jnp.float32
        )
        total[0, first] += term[:, :half]
        total[1, first] += term[:, half:]
        term = jnp.dot(amp[first], along_ref[at], preferred_element_type=jnp.float32)
        total[0, second] += term[:, :half]
        total[1, second] += term[:, half:]


def end_kernel(side, slot_ref, place_ref, *refs):
    pieces, (begun, first_ref, second_ref), refs = refs[:XS], refs[XS : XS + 3], refs[XS + 3 :]
    outs, (amp, total, largest) = refs[:XS], refs[XS:]
    step = pl.program_id(0)
    slots, rows, half = total.shape
    part = rows // YS
    chunks = half // LANES

    @pl.when(step == 0)
    def _():
        lay_out(place_ref, 1, pieces, amp)
        total[...] = begun[place_ref[2] ^ side]

    for at in range(first_ref.shape[0]):
        task = step * first_ref.shape[0] + at
        first = slot_ref[2 * task]
        second = slot_ref[2 * task + 1]
        total[first] += lax.dot_general(
            amp[second], first_ref[at], (((1,), (1,)), ((), ())), preferred_element_type=jnp.float32
        )
        total[second] += jnp.dot(amp[first], second_ref[at], preferred_element_type=jnp.float32)

    @pl.when(step == pl.num_programs(0) - 1)
    def _():
        for far in range(XS):
            spots = [spot(place_ref, side, far, near, part) for near in range(XS)]

            def block_of(block):
                entry, lanes = block // chunks, block % chunks * LANES
                slot, row = spots[entry // ZS]
                return total[slot + entry % ZS, pl.ds(row, part), lanes : lanes + LANES]

            encode(block_of, slots * chunks, outs[far], largest.at[far])


def products(kernel, slots, place, operands, blocks, specs, out_shape, scratch, share):
    tasks, width, _ = blocks.shape
    return pl.pallas_call(
        kernel,
        out_shape=out_shape,
        grid_spec=pltpu.PrefetchScalarGridSpec(
            num_scalar_prefetch=2,
            grid=(tasks // PER_STEP,),
            in_specs=[VMEM] * len(operands) + specs,
            out_specs=jax.tree.map(lambda _: VMEM, out_shape),
            scratch_shapes=scratch,
        ),
        compiler_params=pltpu.CompilerParams(vmem_limit_bytes=LIMIT * MIB),
        cost_estimate=pl.CostEstimate(
            flops=4 * tasks * 128 * width * width // share,
            bytes_accessed=4 * tasks * width * width // share,
            transcendentals=0,
        ),
    )(slots, place, *operands, blocks, blocks)


def begin(slots, place, pieces, blocks):
    entries, part, half = pieces[0].shape
    width = blocks.shape[1]
    specs = [
        pl.BlockSpec((PER_STEP, width, half), lambda t, _, place: (t, 0, place[2])),
        pl.BlockSpec((PER_STEP, half, width), lambda t, _, place: (t, place[2], 0)),
    ]
    out = jax.ShapeDtypeStruct((CORES, entries, YS * part, half), jnp.float32)
    scratch = [pltpu.VMEM((entries, YS * part, half), blocks.dtype)]
    return products(begin_kernel, slots, place, pieces, blocks, specs, out, scratch, 2)


def end(side, slots, place, pieces, begun, blocks):
    entries, part, half = pieces[0].shape
    specs = [
        pl.BlockSpec((PER_STEP, half, half), lambda t, _, place: (t, place[2] ^ side, 1 - place[2])),
        pl.BlockSpec((PER_STEP, half, half), lambda t, _, place: (t, 1 - place[2], place[2] ^ side)),
    ]
    count = entries * (half // LANES)
    out = jax.ShapeDtypeStruct((count + extra(count, part), part, LANES), jnp.int16)
    scratch = [
        pltpu.VMEM((entries, YS * part, half), blocks.dtype),
        pltpu.VMEM((entries, YS * part, half), jnp.float32),
        pltpu.VMEM((XS, extra(count, part) * part, LANES), jnp.float32),
    ]
    operands = [*pieces, begun]
    kernel = functools.partial(end_kernel, side)
    return products(kernel, slots, place, operands, blocks, specs, [out] * XS, scratch, 4)


def combine_kernel(place_ref, want_ref, *refs):
    pieces, outs, totals, largest = refs[: 2 * XS], refs[2 * XS : 3 * XS], refs[3 * XS : -1], refs[-1]
    core = place_ref[2]
    tiles, rows, half = totals[0].shape
    per_owner = tiles // ZS
    chunks = half // LANES
    for total in totals:
        total[...] = jnp.zeros_like(total)
    for side in range(CORES):
        for far in range(XS):
            piece = pieces[side * XS + far]
            row = far * CORES + side
            scales = scale_blocks(piece, XS * ZS * chunks)
            for z in range(ZS):
                for near, total in enumerate(totals):
                    slot = (near + core * (far - near)) * ZS
                    tile = z * per_owner + want_ref[row, slot + z]
                    for chunk in range(chunks):
                        at = (near * ZS + z) * chunks + chunk
                        lanes = slice(chunk * LANES, (chunk + 1) * LANES)
                        total[tile, :, lanes] += numbers(piece[at]) * scales[at]
    for near, total in enumerate(totals):

        def block_of(at):
            return total[at // chunks, :, at % chunks * LANES : (at % chunks + 1) * LANES]

        encode(block_of, tiles * chunks, outs[near], largest.at[near])


def regroup_kernel(*refs):
    pieces, out, largest = refs[:XS], refs[XS], refs[XS + 1]
    rows = out.shape[2]
    count = out.shape[1] - extra(out.shape[1] - 1, rows)
    scales = [scale_blocks(piece, ZS * count) for piece in pieces]
    for z in range(ZS):
        sums = []
        for at in range(z * count, (z + 1) * count):
            sums.append(sum(numbers(piece[at]) * scale[at] for piece, scale in zip(pieces, scales)))
        for core in range(CORES):
            to = z * CORES + core
            encode(lambda at: sums[at][core * rows : (core + 1) * rows], count, out, largest.at[to], (to,))


def finish_kernel(pieces, out):
    per_owner, _, width = out.shape
    chunks = width // CORES // LANES
    scales = [scale_blocks(pieces, per_owner * chunks, (source,)) for source in range(ZS * CORES)]
    for core in range(CORES):
        for which in range(per_owner):
            for chunk in range(chunks):
                at = which * chunks + chunk
                sources = [z * CORES + core for z in range(ZS)]
                found = sum(numbers(pieces[source, at]) * scales[source][at] for source in sources)
                lane = (core * chunks + chunk) * LANES
                out[which, :, lane : lane + LANES] = found


def local(amplitudes, tasks, integrals):
    rows, per_owner, width = amplitudes.shape
    half = width // 2
    entries = XS * ZS
    part = CORES * rows
    kind = amplitudes.dtype
    place = jnp.stack([lax.axis_index(axis) for axis in PLANE]).astype(jnp.int32)
    x = place[0]

    halves = amplitudes.reshape(rows, per_owner, CORES, half).transpose(2, 1, 0, 3)
    halves = jnp.broadcast_to(halves[None], (ZS, *halves.shape)).reshape(-1, *halves.shape[1:])
    along_z = swap(halves, ("z", "core"))
    gathered = [along_z] + [move(along_z, near, True) for near in range(1, XS)]

    names = tasks.reshape(-1)
    owner = names * 171 >> 9
    slots = ((x - (owner // ZS)) & (XS - 1)) * ZS + (owner & (ZS - 1))
    lane = lax.broadcasted_iota(jnp.int32, (names.shape[0], LANES), 1)
    which = (names - owner * per_owner)[:, None]
    want = jnp.max(jnp.where(slots[:, None] == lane, which, 0), axis=0, keepdims=True)
    want = jnp.concatenate([want, trade(want)])
    wants = jnp.concatenate([want] + [move(want, -far, False) for far in range(1, XS)])

    piece = jax.ShapeDtypeStruct((entries, part, half), kind)
    packed = call(pack_kernel, [piece] * (2 * XS), [SMEM] * 2 + [VMEM] * XS)(place, wants, *gathered)
    direct, via = packed[:XS], packed[XS:]
    direct = [v if far == 0 else move(v, far, False) for far, v in enumerate(direct)]
    last, direct[1] = lax.optimization_barrier((via[0], direct[1]))
    via = [trade(last) if far == 0 else move(v, far, False, 1) for far, v in enumerate(via)]

    begun = begin(slots, place, direct, integrals)
    codes = end(0, slots, place, via, begun, integrals)
    onward = end(1, slots, place, via, begun, integrals)
    direct = [v if far == 0 else move(v, -far, False) for far, v in enumerate(codes)]
    via = [trade(v) if far == 0 else move(v, -far, True, 1) for far, v in enumerate(onward)]
    tiles = ZS * per_owner
    chunks = half // LANES
    count = tiles * chunks
    cut = jax.ShapeDtypeStruct((count + extra(count, part), part, LANES), jnp.int16)
    by_near = call(
        combine_kernel,
        [cut] * XS,
        [SMEM] * 2 + [VMEM] * (2 * XS),
        [pltpu.VMEM((tiles, part, half), jnp.float32)] * XS
        + [pltpu.VMEM((XS, extra(count, part) * part, LANES), jnp.float32)],
    )(place, wants, *direct, *via)
    by_near = [v if near == 0 else move(v, -near, True) for near, v in enumerate(by_near)]
    count = per_owner * chunks
    cut = jax.ShapeDtypeStruct((ZS * CORES, count + extra(count, rows), rows, LANES), jnp.int16)
    largest = pltpu.VMEM((ZS * CORES, extra(count, rows) * rows, LANES), jnp.float32)
    by_z = swap(call(regroup_kernel, cut, [VMEM] * XS, [largest])(*by_near), ("z", "core"))
    out = jax.ShapeDtypeStruct((per_owner, rows, width), jnp.float32)
    return call(finish_kernel, out, [VMEM])(by_z).transpose(1, 0, 2)


def solution(mesh):
    fine = Mesh(mesh.devices.reshape(XS, ZS, YS, CORES), ("x", "z", "y", "core"))
    tile, pair = ("x", "z"), ("y", "core")
    return jax.shard_map(
        local,
        mesh=fine,
        in_specs=(P(pair, tile, None), P(tile + pair, None), P(tile + pair, None, None)),
        out_specs=P(pair, tile, None),
        check_vma=False,
    )
```
